32 devices in a mesh: grp: 2 (over x), feat: 16 (over z, y, core).
Axes of the slice: x: 2, y: 2, z: 4, core: 2. Of those that a mesh axis runs over, the one named last changes fastest.
Arguments:
- x_acts: bfloat16 [8, 1024, 4096], P('grp'), parts along dimension 0, may hold values from -6 to 6
- delta: bfloat16 [8, 1024, 4096], P('grp', None, 'feat'), parts along dimension 0, may hold values from -6 to 6
- pattern: int32 [32, 32], replicated, may hold values 0 or 1
- row_signs: int32 [4096], replicated, may hold values from -1 to 1, as said below
- col_signs: int32 [4096], replicated, may hold values from -1 to 1, as said below
- cols: int32 [8192], replicated, may hold values from 0 to 16777215
Outputs:
- sketch: float32 [8, 8192], P('grp'), parts along dimension 0
The draws below stay inside these ranges and needn't reach their ends.
There are 2 independent parts, one for each index of `grp`. The reference program is written for one: setup_inputs(seed, part) draws one part's arguments, and reference() takes and returns one part's arrays. A program takes and returns all parts, laid end to end along the dimension named above; an argument that names none is the same for every part. Nothing has to cross between parts.
Inputs may be any that keep to these rules, and one draw needn't show every extreme that they name: `row_signs`: every entry is -1 or +1. `col_signs`: every entry is -1 or +1.
All inputs are finite; a program needn't handle non-finite values.
Results may differ from the reference program's by a relative error of at most 0.0029.
Values may be sent and summed in bfloat16 or wider, within the bound.
A program may use at most 192 MiB of HBM per device.

```python
import math
import jax
import jax.numpy as jnp
from jax import lax

D_IN = 4096
D_OUT = 4096
BLK = 128
SKETCH = 8192
EX = 4
TOK = 1024


def draw_row_signs(key, part):
    coin_bits = jax.random.randint(jax.random.fold_in(key, 11), (D_OUT,), 0, 2)
    return (2 * coin_bits - 1).astype(jnp.int32)


def draw_col_signs(key, part):
    coin_bits = jax.random.randint(jax.random.fold_in(key, 23), (D_IN,), 0, 2)
    return (2 * coin_bits - 1).astype(jnp.int32)


def plant(array, stream_key, least, largest):
    longest = array.shape.index(max(array.shape))
    spots = []
    for shift in (0, 1):
        where = [jax.random.randint(jax.random.fold_in(stream_key, axis), (), 0, length) for axis, length in enumerate(array.shape)]
        where[longest] = (where[longest] + shift) % array.shape[longest]
        spots.append(tuple(where))
    return array.at[spots[0]].set(least).at[spots[1]].set(largest)


def steps_of(stream_key, dims, split, smallest, high):
    loudness, own = 1.0, jax.random.fold_in(stream_key, 6)
    for position, shards_of in split:
        heights = jnp.exp(jax.random.uniform(jax.random.fold_in(own, position), (shards_of,), jnp.float32, smallest / len(split), high / len(split)))
        loudness = loudness * jnp.repeat(heights, dims[position] // shards_of).reshape([-1 if axis == position else 1 for axis in range(len(dims))])
    return loudness


def normal_values(own_key, extent, width, reach, split=(), dtype=jnp.bfloat16):
    result = jax.random.normal(own_key, extent, jnp.float32) * width
    if len(split) > 0:
        result = steps_of(own_key, extent, split, -0.22, 0.18) * result
    return jnp.clip(result, min=-reach, max=reach).astype(dtype)


def setup_inputs(seed: int = 0, part: int = 0) -> dict:
    streams_of = jax.random.split(jax.random.key(seed), 7)
    part_splits = jax.random.split(jax.random.fold_in(streams_of[6], part), 7)
    x_acts = normal_values(part_splits[0], (EX, TOK, D_IN), 1.0, 6.0)
    delta = normal_values(part_splits[1], (EX, TOK, D_OUT), 1.0, 6.0, ((2, 16),))
    pattern = plant((jax.random.randint(streams_of[2], (D_OUT // BLK, D_IN // BLK), 0, 2) < 1).astype(jnp.int32), jax.random.fold_in(streams_of[2], 1), 0, 1)
    row_signs = draw_row_signs(jax.random.fold_in(streams_of[6], 71), part)
    col_signs = draw_col_signs(jax.random.fold_in(streams_of[6], 71), part)
    cols = plant(jax.random.randint(streams_of[5], (SKETCH,), 0, D_OUT * D_IN), jax.random.fold_in(streams_of[5], 1), 0, (D_OUT * D_IN) - 1).astype(jnp.int32)
    return dict(x_acts=x_acts, delta=delta, pattern=pattern, row_signs=row_signs, col_signs=col_signs, cols=cols)


def walsh_transform(values, axis_pos):
    values = jnp.moveaxis(values, axis_pos, -1)
    length = values.shape[-1]
    leading = values.shape[:-1]
    half_len = 1
    while half_len < length:
        blocks = values.reshape(leading + (length // (2 * half_len), 2, half_len))
        lower = blocks[..., 0, :]
        upper = blocks[..., 1, :]
        values = jnp.stack([lower + upper, lower - upper], axis=-2).reshape(leading + (length,))
        half_len = half_len * 2
    return jnp.moveaxis(values, -1, axis_pos)

def reference(x_acts, delta, pattern, row_signs, col_signs, cols):
    block_mask = jnp.repeat(jnp.repeat(pattern, BLK, axis=0), BLK, axis=1).astype(jnp.float32)
    sign_values = (row_signs[:, None] * col_signs[None, :]).astype(jnp.float32)

    def one_example(inputs):
        acts_one, delta_one = inputs
        gradient = jnp.dot(delta_one.T, acts_one, preferred_element_type=jnp.float32) / TOK
        gradient = (gradient * block_mask).astype(jnp.bfloat16)
        signed = gradient.astype(jnp.float32) * sign_values
        transformed = walsh_transform(walsh_transform(signed, 1), 0)
        return transformed.reshape(-1)[cols] / math.sqrt(SKETCH)
    return lax.map(one_example, (x_acts, delta))
```

```python
import functools
import math

import jax
import jax.numpy as jnp
from jax import lax
from jax.experimental import pallas as pl
from jax.experimental.pallas import tpu as pltpu
from jax.sharding import PartitionSpec as P

BLK = 128
LANES = 128
TILE = 256
CHUNK = 512
F32 = jnp.float32
BF16 = jnp.bfloat16
NT = (((1,), (1,)), ((), ()))


def parity(value, bits):
    shift = 1
    while shift < bits:
        shift *= 2
    while shift > 1:
        shift //= 2
        value = value ^ (value >> shift)
    return value & 1


def sign_of(left, right, bits):
    return (1 - 2 * parity(left & right, bits)).astype(F32)


def iota(shape, axis):
    return lax.broadcasted_iota(jnp.int32, shape, axis)


def plan(cols_ref, tp_ref, lp_ref, rc_ref, info_v, info_s, rank_ref, sem, bins, width, rows, tiles):
    n_rows = cols_ref.shape[0]
    before = (iota((TILE, TILE), 0) < iota((TILE, TILE), 1)).astype(F32).astype(BF16)
    every = jnp.ones((TILE, TILE), BF16)
    bin_ids = iota((bins, TILE), 0)

    def hits(a):
        block = (cols_ref[pl.ds(a, 1), :] % width) // LANES
        return (bin_ids == block).astype(F32)

    def count(a, running):
        hit = hits(a)
        hit16 = hit.astype(BF16)
        ahead = jnp.dot(hit16, before, preferred_element_type=F32)
        total = jnp.dot(hit16, every, preferred_element_type=F32)
        rank = jnp.sum(hit * (ahead + running), axis=0, keepdims=True)
        rank_ref[pl.ds(a, 1), :] = rank.astype(jnp.int32)
        return running + total

    counts = lax.fori_loop(0, n_rows, count, jnp.zeros((bins, TILE), F32), unroll=8)
    need = (counts.astype(jnp.int32) + (TILE - 1)) // TILE
    lower = (iota((bins, bins), 1) < iota((bins, bins), 0)).astype(F32).astype(BF16)
    start = jnp.dot(lower, need.astype(F32).astype(BF16), preferred_element_type=F32)
    ends = start.astype(jnp.int32) + need
    tile_ids = iota((bins, LANES), 1)
    owner = jnp.sum((ends[:, :LANES] <= tile_ids).astype(jnp.int32), axis=0, keepdims=True)
    owner = jnp.minimum(owner, bins - 1)
    used = ends[bins - 1 :, :LANES]
    info_v[...] = jnp.where(iota((8, LANES), 0) == 0, owner, used)
    copy = pltpu.make_async_copy(info_v, info_s, sem)
    copy.start()

    slots = 2 * tiles
    slot_ids = iota((slots, TILE), 0)
    lane_ids = iota((LANES, TILE), 0)

    def place(a, acc):
        first = jnp.sum(hits(a) * start, axis=0, keepdims=True).astype(jnp.int32)
        rank = rank_ref[pl.ds(a, 1), :]
        lane = rank % TILE
        slot = first + rank // TILE + (lane // LANES) * tiles
        lane = lane % LANES
        tp_ref[pl.ds(a, 1), :] = slot
        lp_ref[pl.ds(a, 1), :] = lane
        cols = cols_ref[pl.ds(a, 1), :]
        row = ((cols // width) % rows).astype(F32)
        col = (cols % LANES).astype(F32)
        here = slot_ids == slot
        left = jnp.concatenate([jnp.where(here, row, 0.0), jnp.where(here, col, 0.0)], axis=0)
        right = (lane_ids == lane).astype(F32)
        return acc + lax.dot_general(
            left.astype(BF16), right.astype(BF16), NT, preferred_element_type=F32
        )

    acc = lax.fori_loop(0, n_rows, place, jnp.zeros((2 * slots, LANES), F32), unroll=4)
    acc = acc.astype(jnp.int32)
    for v in range(2):
        part = acc[v * slots : (v + 1) * slots]
        rc_ref[v] = jnp.concatenate([part[:tiles], part[tiles:]], axis=1)
    copy.wait()


def butterfly(g_ref, bins):
    def slab(s, carry):
        rows = pl.ds(pl.multiple_of(s * 8, 8), 8)
        parts = [g_ref[rows, c * LANES : (c + 1) * LANES] for c in range(bins)]
        half = 1
        while half < bins:
            for c in range(bins):
                if not c & half:
                    low, high = parts[c], parts[c + half]
                    parts[c], parts[c + half] = low + high, low - high
            half *= 2
        for c in range(bins):
            g_ref[rows, c * LANES : (c + 1) * LANES] = parts[c]
        return carry

    lax.fori_loop(0, g_ref.shape[0] // 8, slab, 0)


def tile_values(t, rc_ref, info_s, t1_ref, so_ref):
    examples, _, rows = t1_ref.shape[1:]
    row = rc_ref[0, pl.ds(t, 1), :]
    col = rc_ref[1, pl.ds(t, 1), :]
    low_ids = iota((16, TILE), 0)
    row_low = sign_of(low_ids, row % 16, 4).astype(BF16)
    high_bits = rows // 16
    row_high = sign_of(iota((max(high_bits, 8), TILE), 0), row // 16, 8).astype(BF16)
    weight = jnp.concatenate([row_low * row_high[h : h + 1] for h in range(high_bits)], axis=0)
    block = t1_ref[info_s[0, t]].reshape(examples * LANES, rows)
    value = jnp.dot(block, weight, preferred_element_type=F32)
    col_low = sign_of(iota((8, TILE), 0), col % 8, 3)
    col_high = sign_of(iota((16, TILE), 0), col // 8, 4)
    for e in range(examples):
        total = jnp.zeros((8, TILE), F32)
        for h in range(16):
            at = e * LANES + h * 8
            total = total + value[at : at + 8] * col_high[h : h + 1]
        so_ref[e, pl.ds(t, 1), :] = jnp.sum(total * col_low, axis=0, keepdims=True)


def unplace(me, cols_ref, tp_ref, lp_ref, so_ref, out_ref, width, rows, tiles):
    examples = so_ref.shape[0]
    flipped = []
    for e in range(examples):
        one = so_ref[e]
        both = jnp.concatenate([one[:, :LANES], one[:, LANES:]], axis=0)
        flipped.append(both.T)
    table = jnp.concatenate(flipped, axis=0).astype(BF16)
    slot_ids = iota((2 * tiles, CHUNK), 0)
    lane_ids = iota((LANES, CHUNK), 0)

    def wide(ref, a):
        return jnp.concatenate([ref[pl.ds(2 * a, 1), :], ref[pl.ds(2 * a + 1, 1), :]], axis=1)

    def chunk(a, carry):
        pick = (slot_ids == wide(tp_ref, a)).astype(F32).astype(BF16)
        spread = jnp.dot(table, pick, preferred_element_type=F32)
        mine = lane_ids == wide(lp_ref, a)
        high = wide(cols_ref, a) // (width * rows)
        sign = sign_of(high, me, 16)
        kept = [
            jnp.sum(jnp.where(mine, spread[e * LANES : (e + 1) * LANES], 0.0), axis=0, keepdims=True) * sign
            for e in range(examples)
        ]
        lines = [
            kept[e][:, q * LANES : (q + 1) * LANES]
            for q in range(CHUNK // LANES)
            for e in range(examples)
        ]
        out_ref[a] = jnp.concatenate(lines, axis=0).astype(BF16)
        return carry

    lax.fori_loop(0, out_ref.shape[0], chunk, 0, unroll=2)


def sketch_kernel(
    bins, tiles, me_ref, x_ref, delta_ref, rs_ref, cf_ref, cols_ref, out_ref,
    dt_ref, g_ref, t1_ref, tp_ref, lp_ref, rank_ref, rc_ref, so_ref, info_v, info_s, sem,
):
    e, nb = pl.program_id(0), pl.program_id(1)
    rows, width = g_ref.shape
    step_cols = x_ref.shape[2]

    @pl.when((e == 0) & (nb == 0))
    def _():
        plan(cols_ref, tp_ref, lp_ref, rc_ref, info_v, info_s, rank_ref, sem, bins, width, rows, tiles)

    @pl.when(nb == 0)
    def _():
        dt_ref[...] = (delta_ref[0] * rs_ref[...]).T

    acc = jnp.dot(dt_ref[...], x_ref[0], preferred_element_type=F32)
    at = pl.ds(pl.multiple_of(nb * step_cols, step_cols), step_cols)
    per = min(rows, BLK)
    for b in range(rows // per):
        part = acc[b * per : (b + 1) * per] * cf_ref[b : b + 1, :]
        g_ref[b * per : (b + 1) * per, at] = part.astype(BF16).astype(F32)

    @pl.when(nb == pl.num_programs(1) - 1)
    def _():
        butterfly(g_ref, bins)
        for c in range(bins):
            t1_ref[c, e] = g_ref[:, c * LANES : (c + 1) * LANES].astype(BF16).T

    @pl.when((e == pl.num_programs(0) - 1) & (nb == pl.num_programs(1) - 1))
    def _():
        so_ref[...] = jnp.zeros_like(so_ref)

        def four(s, carry):
            for u in range(4):
                tile_values(s * 4 + u, rc_ref, info_s, t1_ref, so_ref)
            return carry

        lax.fori_loop(0, (info_s[1, 0] + 3) // 4, four, 0)
        unplace(me_ref[0], cols_ref, tp_ref, lp_ref, so_ref, out_ref, width, rows, tiles)


def local_sketch(me, x_acts, delta, row_sign, col_factor, cols):
    examples, tokens, width = x_acts.shape
    rows = delta.shape[2]
    sketch = cols.shape[0]
    bins = width // LANES
    tiles = sketch // TILE + bins
    step_cols = 1024
    smem = pl.BlockSpec(memory_space=pltpu.SMEM)
    whole = lambda shape: pl.BlockSpec(shape, lambda e, n: (0,) * len(shape))
    lines = CHUNK // LANES * examples
    out_shape = (sketch // CHUNK, lines, LANES)
    return pl.pallas_call(
        functools.partial(sketch_kernel, bins, tiles),
        grid=(examples, width // step_cols),
        out_shape=jax.ShapeDtypeStruct(out_shape, BF16),
        in_specs=[
            smem,
            pl.BlockSpec((1, tokens, step_cols), lambda e, n: (e, 0, n)),
            pl.BlockSpec((1, tokens, rows), lambda e, n: (e, 0, 0)),
            whole((1, rows)),
            pl.BlockSpec((col_factor.shape[0], step_cols), lambda e, n: (0, n)),
            whole((sketch // TILE, TILE)),
        ],
        out_specs=whole(out_shape),
        scratch_shapes=[
            pltpu.VMEM((rows, tokens), BF16),
            pltpu.VMEM((rows, width), F32),
            pltpu.VMEM((bins, examples, LANES, rows), BF16),
            pltpu.VMEM((sketch // TILE, TILE), jnp.int32),
            pltpu.VMEM((sketch // TILE, TILE), jnp.int32),
            pltpu.VMEM((sketch // TILE, TILE), jnp.int32),
            pltpu.VMEM((2, tiles, TILE), jnp.int32),
            pltpu.VMEM((examples, tiles, TILE), F32),
            pltpu.VMEM((8, LANES), jnp.int32),
            pltpu.SMEM((8, LANES), jnp.int32),
            pltpu.SemaphoreType.DMA,
        ],
        compiler_params=pltpu.CompilerParams(vmem_limit_bytes=48 * 2**20),
        cost_estimate=pl.CostEstimate(
            flops=2 * examples * tokens * width * rows,
            bytes_accessed=2 * examples * tokens * (width + rows),
            transcendentals=0,
        ),
    )(me, x_acts, delta, row_sign, col_factor, cols.reshape(sketch // TILE, TILE))


def sum_kernel(n, part_ref, out_ref, recv, send1, recv1, send2, recv2):
    me = lax.axis_index("feat")
    barrier = pltpu.get_barrier_semaphore()

    def other(o):
        return lax.rem(me + o, n)

    def greet(o, carry):
        pl.semaphore_signal(
            barrier, inc=1, device_id={"feat": other(o)}, device_id_type=pl.DeviceIdType.MESH
        )
        return carry

    lax.fori_loop(1, n, greet, 0)
    pl.semaphore_wait(barrier, n - 1)

    def share(src, dst, send_sem, recv_sem, to):
        return pltpu.make_async_remote_copy(
            src_ref=src,
            dst_ref=dst,
            send_sem=send_sem,
            recv_sem=recv_sem,
            device_id={"feat": to},
            device_id_type=pl.DeviceIdType.MESH,
        )

    def scatter(o, start):
        to, source = other(o), other(n - o)
        copy = share(part_ref.at[to], recv.at[me], send1.at[to], recv1.at[me], to)
        if start:
            copy.start()
        else:
            copy.wait_send()
            share(part_ref.at[source], recv.at[source], send1.at[source], recv1.at[source], source).wait_recv()

    def gather(o, start):
        to, source = other(o), other(n - o)
        copy = share(out_ref.at[me], out_ref.at[me], send2.at[to], recv2.at[me], to)
        if start:
            copy.start()
        else:
            copy.wait_send()
            share(out_ref.at[source], out_ref.at[source], send2.at[source], recv2.at[source], source).wait_recv()

    def each(step, start):
        def body(o, carry):
            step(o, start)
            return carry

        lax.fori_loop(1, n, body, 0)

    each(scatter, True)
    each(scatter, False)
    recv[me] = part_ref[me]
    total = recv[0].astype(F32)
    for s in range(1, n):
        total = total + recv[s].astype(F32)
    out_ref[me] = total.astype(out_ref.dtype)
    each(gather, True)
    each(gather, False)


def sum_shares(parts, n):
    vmem = pl.BlockSpec(memory_space=pltpu.VMEM)
    return pl.pallas_call(
        functools.partial(sum_kernel, n),
        out_shape=jax.ShapeDtypeStruct(parts.shape, BF16),
        in_specs=[vmem],
        out_specs=vmem,
        scratch_shapes=[pltpu.VMEM(parts.shape, BF16)] + [pltpu.SemaphoreType.DMA((n,))] * 4,
        compiler_params=pltpu.CompilerParams(collective_id=0, has_side_effects=True),
    )(parts)


def per_device(x_acts, delta, pattern, row_signs, col_signs, cols):
    examples, tokens, width = x_acts.shape
    rows = delta.shape[2]
    sketch = cols.shape[0]
    n = lax.axis_size("feat")
    me = lax.axis_index("feat")
    row_sign = lax.dynamic_slice_in_dim(row_signs, me * rows, rows).astype(BF16)[None]
    bands = max(rows // BLK, 1)
    band = lax.dynamic_slice_in_dim(pattern, me * rows // BLK, bands, 0)
    factor = jnp.repeat(band, BLK, axis=1) * col_signs[None]
    col_factor = factor.astype(F32) / tokens
    parts = local_sketch(me[None], x_acts, delta, row_sign, col_factor, cols)
    shape = parts.shape
    total = sum_shares(parts.reshape(n, parts.size // n // LANES, LANES), n).reshape(shape)
    total = total.reshape(shape[0], CHUNK // LANES, examples, LANES).transpose(2, 0, 1, 3)
    return total.reshape(examples, sketch).astype(F32) / math.sqrt(sketch)


def solution(mesh):
    placed = (P("grp", None, None), P("grp", None, "feat"), P(), P(), P(), P())
    return jax.shard_map(
        per_device, mesh=mesh, in_specs=placed, out_specs=P("grp", None), check_vma=False
    )
```

```python
import functools
import math

import jax
import jax.numpy as jnp
from jax import lax
from jax.experimental import pallas as pl
from jax.experimental.pallas import tpu as pltpu
from jax.sharding import PartitionSpec as P

BLK = 128
LANES = 128
TILE = 256
CHUNK = 512
F32 = jnp.float32
BF16 = jnp.bfloat16
NT = (((1,), (1,)), ((), ()))


def parity(value, bits):
    shift = 1
    while shift < bits:
        shift *= 2
    while shift > 1:
        shift //= 2
        value = value ^ (value >> shift)
    return value & 1


def sign_of(left, right, bits):
    return (1 - 2 * parity(left & right, bits)).astype(F32)


def iota(shape, axis):
    return lax.broadcasted_iota(jnp.int32, shape, axis)


def hits(cols_ref, a, bins, width):
    block = (cols_ref[:, pl.ds(pl.multiple_of(a * TILE, TILE), TILE)] % width) // LANES
    return iota((bins, TILE), 0) == block


def count(cols_ref, rank_ref, start_ref, info_v, bins, width):
    n_rows = cols_ref.shape[1] // TILE
    before = (iota((TILE, 2 * TILE), 0) < iota((TILE, 2 * TILE), 1)).astype(F32).astype(BF16)
    hit = [hits(cols_ref, a, bins, width).astype(F32) for a in range(n_rows)]
    ahead = jnp.dot(
        jnp.concatenate(hit, axis=0).astype(BF16), before, preferred_element_type=F32
    )
    running = jnp.zeros((bins, TILE), F32)
    for a in range(n_rows):
        here = ahead[a * bins : (a + 1) * bins]
        rank = jnp.sum(hit[a] * (here[:, :TILE] + running), axis=0, keepdims=True)
        rank_ref[a : a + 1, :] = rank.astype(jnp.int32)
        running = running + here[:, TILE:]
    need = (running.astype(jnp.int32) + (TILE - 1)) // TILE
    lower = (iota((bins, bins), 1) < iota((bins, bins), 0)).astype(F32).astype(BF16)
    start = jnp.dot(lower, need.astype(F32).astype(BF16), preferred_element_type=F32)
    start_ref[...] = start
    ends = start.astype(jnp.int32) + need
    tile_ids = iota((bins, LANES), 1)
    owner = jnp.sum((ends[:, :LANES] <= tile_ids).astype(jnp.int32), axis=0, keepdims=True)
    owner = jnp.minimum(owner, bins - 1)
    used = ends[bins - 1 :, :LANES]
    info_v[...] = jnp.where(iota((8, LANES), 0) == 0, owner, used)


def place(a, cols_ref, rank_ref, start_ref, tp_ref, lp_ref, bins, width, rows, tiles):
    slots = 2 * tiles
    first = jnp.sum(
        jnp.where(hits(cols_ref, a, bins, width), start_ref[...], 0.0), axis=0, keepdims=True
    )
    rank = rank_ref[pl.ds(a, 1), :]
    lane = rank % TILE
    slot = first.astype(jnp.int32) + rank // TILE + (lane // LANES) * tiles
    lane = lane % LANES
    tp_ref[pl.ds(a, 1), :] = slot
    lp_ref[pl.ds(a, 1), :] = lane
    cols = cols_ref[:, pl.ds(pl.multiple_of(a * TILE, TILE), TILE)]
    row = ((cols // width) % rows).astype(F32)
    col = (cols % LANES).astype(F32)
    here = iota((slots, TILE), 0) == slot
    left = jnp.concatenate([jnp.where(here, row, 0.0), jnp.where(here, col, 0.0)], axis=0)
    right = (iota((LANES, TILE), 0) == lane).astype(F32)
    return lax.dot_general(
        left.astype(BF16), right.astype(BF16), NT, preferred_element_type=F32
    )


def stages(parts, first, last):
    half = first
    while half < last:
        for c in range(len(parts)):
            if not c & half:
                low, high = parts[c], parts[c + half]
                parts[c], parts[c + half] = low + high, low - high
        half *= 2
    return parts


def butterfly(g_ref, t1_ref, work_ref, slot, e, step, steps):
    bins, lanes, rows = g_ref.shape[1:]
    share = lanes // steps
    wide = min(rows, LANES)
    unit = 0
    for j in range(share // 16):
        at = pl.ds(pl.multiple_of(step * share + j * 16, 16), 16)
        for h in range(rows // wide):
            span = slice(h * wide, (h + 1) * wide)
            inner = 8 if bins % 8 == 0 else bins
            for c0 in range(0, bins, inner):
                parts = [g_ref[slot, c0 + c, at, span].astype(F32) for c in range(inner)]
                for c, part in enumerate(stages(parts, 1, inner)):
                    work_ref[unit, c0 + c] = part
            for c0 in range(inner):
                parts = [work_ref[unit, c] for c in range(c0, bins, inner)]
                for c, part in enumerate(stages(parts, 1, len(parts))):
                    t1_ref[c0 + c * inner, e, at, span] = part.astype(BF16)
            unit += 1


def tile_values(t, rc_ref, info_s, t1_ref, so_ref):
    examples, _, rows = t1_ref.shape[1:]
    row = rc_ref[0, pl.ds(t, 1), :]
    col = rc_ref[1, pl.ds(t, 1), :]
    low_ids = iota((16, TILE), 0)
    row_low = sign_of(low_ids, row % 16, 4).astype(BF16)
    high_bits = rows // 16
    row_high = sign_of(iota((max(high_bits, 8), TILE), 0), row // 16, 8).astype(BF16)
    weight = jnp.concatenate([row_low * row_high[h : h + 1] for h in range(high_bits)], axis=0)
    block = t1_ref[info_s[0, t]].reshape(examples * LANES, rows)
    value = jnp.dot(block, weight, preferred_element_type=F32)
    col_low = sign_of(iota((8, TILE), 0), col % 8, 3)
    col_high = sign_of(iota((16, TILE), 0), col // 8, 4)
    for e in range(examples):
        total = jnp.zeros((8, TILE), F32)
        for h in range(16):
            at = e * LANES + h * 8
            total = total + value[at : at + 8] * col_high[h : h + 1]
        so_ref[e, pl.ds(t, 1), :] = jnp.sum(total * col_low, axis=0, keepdims=True)


def entries(a, me, table_ref, tp_ref, lp_ref, cols_ref, n_examples, chunk, width, rows):
    per = chunk // TILE

    def wide(ref):
        return jnp.concatenate([ref[pl.ds(per * a + u, 1), :] for u in range(per)], axis=1)

    pick = (iota((table_ref.shape[1], chunk), 0) == wide(tp_ref)).astype(F32).astype(BF16)
    spread = jnp.dot(table_ref[...], pick, preferred_element_type=F32)
    mine = iota((LANES, chunk), 0) == wide(lp_ref)
    high = cols_ref[:, pl.ds(pl.multiple_of(a * chunk, chunk), chunk)] // (width * rows)
    sign = sign_of(high, me, 16)
    kept = [
        jnp.sum(jnp.where(mine, spread[e * LANES : (e + 1) * LANES], 0.0), axis=0, keepdims=True)
        * sign
        for e in range(n_examples)
    ]
    lines = [
        kept[e][:, q * LANES : (q + 1) * LANES]
        for q in range(chunk // LANES)
        for e in range(n_examples)
    ]
    return jnp.concatenate(lines, axis=0).astype(BF16)


def sketch_kernel(
    tiles, me_ref, x_ref, delta_ref, pattern_ref, rs_ref, cs_ref, cols_ref, table_ref, tp_ref, lp_ref,
    dt_ref, cf_ref, g_ref, t1_ref, work_ref, rank_ref, start_ref, pacc_ref, rc_ref, so_ref,
    info_v, info_s, sem,
):
    e, nb = pl.program_id(0), pl.program_id(1)
    examples, steps = pl.num_programs(0), pl.num_programs(1)
    bins, lanes, rows = g_ref.shape[1:]
    n_examples, n_steps = t1_ref.shape[1], cf_ref.shape[0]
    width = bins * lanes
    tokens, step_cols = x_ref.shape[1:]
    bands = cf_ref.shape[1]
    step_blocks = step_cols // LANES
    step = e * n_steps + nb
    n_rows = rank_ref.shape[0]
    me = me_ref[0]

    @pl.when(step == 0)
    def _():
        count(cols_ref, rank_ref, start_ref, info_v, bins, width)
        copy = pltpu.make_async_copy(info_v, info_s, sem)
        copy.start()
        pacc_ref[...] = jnp.zeros_like(pacc_ref)
        so_ref[...] = jnp.zeros_like(so_ref)
        for b in range(bands):
            band = pattern_ref[pl.ds(me * rows // BLK + b, 1), :]
            for c in range(width // BLK):
                at = (c * BLK) % step_cols
                factor = band[:, c : c + 1] * cs_ref[:, c * BLK : (c + 1) * BLK]
                cf_ref[c * BLK // step_cols, b : b + 1, at : at + BLK] = factor.astype(F32) / tokens
        copy.wait()

    @pl.when(nb == 0)
    def _():
        span = max(rows, LANES)
        window = rs_ref[:, pl.ds(pl.multiple_of(me * rows // span * span, span), span)]
        own = window[:, :rows]
        for u in range(1, span // rows):
            own = jnp.where(me % (span // rows) == u, window[:, u * rows : (u + 1) * rows], own)
        dt_ref[...] = (delta_ref[0] * own.astype(F32).astype(BF16)).T

    slot = lax.rem(e, 2)
    last = lax.rem(e + n_examples - 1, n_examples)
    butterfly(g_ref, t1_ref, work_ref, 1 - slot, last, nb, n_steps)

    per_step = -(-n_rows // (n_examples * n_steps))
    for u in range(per_step):
        pacc_ref[...] += place(
            step * per_step + u, cols_ref, rank_ref, start_ref, tp_ref, lp_ref, bins, width, rows, tiles
        )

    acc = jnp.dot(dt_ref[...], x_ref[0], preferred_element_type=F32)
    per = min(rows, BLK)
    factor = cf_ref[nb]
    for c in range(step_blocks):
        span = slice(c * LANES, (c + 1) * LANES)
        block = [
            (acc[b * per : (b + 1) * per, span] * factor[b : b + 1, span]).astype(BF16)
            for b in range(rows // per)
        ]
        g_ref[slot, nb * step_blocks + c] = jnp.concatenate(block, axis=0).T

    @pl.when(step == examples * steps - 1)
    def _():
        for q in range(n_steps):
            butterfly(g_ref, t1_ref, work_ref, slot, e, q, n_steps)
        for v in range(2):
            part = pacc_ref[2 * tiles * v : 2 * tiles * (v + 1)].astype(jnp.int32)
            rc_ref[v] = jnp.concatenate([part[:tiles], part[tiles:]], axis=1)

        def four(s, carry):
            for u in range(4):
                tile_values(s * 4 + u, rc_ref, info_s, t1_ref, so_ref)
            return carry

        lax.fori_loop(0, (info_s[1, 0] + 3) // 4, four, 0)
        for k in range(n_examples):
            one = so_ref[k]
            both = jnp.concatenate([one[:, :LANES], one[:, LANES:]], axis=0)
            table_ref[k * LANES : (k + 1) * LANES] = both.T.astype(BF16)


def local_sketch(me, x_acts, delta, pattern, row_signs, col_signs, cols):
    examples, tokens, width = x_acts.shape
    rows = delta.shape[2]
    sketch = cols.shape[1]
    bins = width // LANES
    tiles = sketch // TILE + bins
    step_cols = 1024
    steps = width // step_cols
    n_rows = sketch // TILE
    bands = max(rows // BLK, 1)
    smem = pl.BlockSpec(memory_space=pltpu.SMEM)
    whole = lambda shape: pl.BlockSpec(shape, lambda e, n: (0,) * len(shape))
    units = LANES // steps // 16 * max(rows // LANES, 1)
    table = (examples * LANES, 2 * tiles)
    places = (n_rows, TILE)
    return pl.pallas_call(
        functools.partial(sketch_kernel, tiles),
        grid=(examples, steps),
        out_shape=[
            jax.ShapeDtypeStruct(table, BF16),
            jax.ShapeDtypeStruct(places, jnp.int32),
            jax.ShapeDtypeStruct(places, jnp.int32),
        ],
        in_specs=[
            smem,
            pl.BlockSpec((1, tokens, step_cols), lambda e, n: (e, 0, n)),
            pl.BlockSpec((1, tokens, rows), lambda e, n: (e, 0, 0)),
            whole(pattern.shape),
            whole(row_signs.shape),
            whole(col_signs.shape),
            whole(cols.shape),
        ],
        out_specs=[whole(table), whole(places), whole(places)],
        scratch_shapes=[
            pltpu.VMEM((rows, tokens), BF16),
            pltpu.VMEM((steps, bands, step_cols), F32),
            pltpu.VMEM((2, bins, LANES, rows), BF16),
            pltpu.VMEM((bins, examples, LANES, rows), BF16),
            pltpu.VMEM((units, bins, 16, min(rows, LANES)), F32),
            pltpu.VMEM(places, jnp.int32),
            pltpu.VMEM((bins, TILE), F32),
            pltpu.VMEM((4 * tiles, LANES), F32),
            pltpu.VMEM((2, tiles, TILE), jnp.int32),
            pltpu.VMEM((examples, tiles, TILE), F32),
            pltpu.VMEM((8, LANES), jnp.int32),
            pltpu.SMEM((8, LANES), jnp.int32),
            pltpu.SemaphoreType.DMA,
        ],
        compiler_params=pltpu.CompilerParams(vmem_limit_bytes=60 * 2**20),
        cost_estimate=pl.CostEstimate(
            flops=2 * examples * tokens * width * rows,
            bytes_accessed=2 * examples * tokens * (width + rows),
            transcendentals=0,
        ),
    )(me, x_acts, delta, pattern, row_signs, col_signs, cols)


def sum_kernel(
    n, n_examples, chunk, width, rows, table_ref, tp_ref, lp_ref, cols_ref, out_ref,
    part, recv, send1, recv1, send2, recv2,
):
    me = lax.axis_index("feat")
    chunks = cols_ref.shape[1] // chunk
    pieces = n // chunks
    lines = part.shape[1]
    barrier = pltpu.get_barrier_semaphore()

    def other(o):
        return lax.rem(me + o, n)

    def loop(first, last, step):
        def body(o, carry):
            step(o)
            return carry

        lax.fori_loop(first, last, body, 0)

    def greet(o):
        pl.semaphore_signal(
            barrier, inc=1, device_id={"feat": other(o)}, device_id_type=pl.DeviceIdType.MESH
        )

    def share(src, dst, send_sem, recv_sem, to):
        return pltpu.make_async_remote_copy(
            src_ref=src,
            dst_ref=dst,
            send_sem=send_sem,
            recv_sem=recv_sem,
            device_id={"feat": to},
            device_id_type=pl.DeviceIdType.MESH,
        )

    def chunk_at(o):
        return lax.rem(me // pieces + 1 + o, chunks)

    def compute(o):
        a = chunk_at(o)
        found = entries(
            a, me, table_ref, tp_ref, lp_ref, cols_ref, n_examples, chunk, width, rows
        )
        for p in range(pieces):
            part[a * pieces + p] = found[p * lines : (p + 1) * lines]

    def send(o):
        for p in range(pieces):
            to = chunk_at(o) * pieces + p

            @pl.when(to != me)
            def _():
                share(part.at[to], recv.at[me], send1.at[to], recv1.at[me], to).start()

    def step(o):
        compute(o)
        send(o)

    loop(1, n, greet)
    compute(0)
    pl.semaphore_wait(barrier, n - 1)
    send(0)
    loop(1, chunks, step)

    def collect(o, total):
        source = other(n - o)
        share(part.at[source], recv.at[source], send1.at[source], recv1.at[source], source).wait_recv()
        return total + recv[source].astype(F32)

    out_ref[me] = lax.fori_loop(1, n, collect, part[me].astype(F32))

    def spread(o):
        to = other(o)
        share(out_ref.at[me], out_ref.at[me], send2.at[to], recv2.at[me], to).start()

    loop(1, n, spread)

    def finish(o):
        to, source = other(o), other(n - o)
        share(part.at[to], recv.at[me], send1.at[to], recv1.at[me], to).wait_send()
        share(out_ref.at[me], out_ref.at[me], send2.at[to], recv2.at[me], to).wait_send()
        share(out_ref.at[source], out_ref.at[source], send2.at[source], recv2.at[source], source).wait_recv()

    loop(1, n, finish)


def sum_shares(table, slots, places, cols, n, examples, chunk, width, rows):
    vmem = pl.BlockSpec(memory_space=pltpu.VMEM)
    shape = (n, cols.shape[1] // n * examples // LANES, LANES)
    return pl.pallas_call(
        functools.partial(sum_kernel, n, examples, chunk, width, rows),
        out_shape=jax.ShapeDtypeStruct(shape, F32),
        in_specs=[vmem] * 4,
        out_specs=vmem,
        scratch_shapes=[pltpu.VMEM(shape, BF16)] * 2 + [pltpu.SemaphoreType.DMA((n,))] * 4,
        compiler_params=pltpu.CompilerParams(
            collective_id=0, has_side_effects=True, vmem_limit_bytes=32 * 2**20
        ),
    )(table, slots, places, cols)


def per_device(x_acts, delta, pattern, row_signs, col_signs, cols):
    examples, tokens, width = x_acts.shape
    rows = delta.shape[2]
    sketch = cols.shape[0]
    n = lax.axis_size("feat")
    me = lax.axis_index("feat")
    chunk = max(sketch // n, CHUNK)
    cols = cols[None]
    table, slots, places = local_sketch(
        me[None], x_acts, delta, pattern, row_signs[None], col_signs[None], cols
    )
    total = sum_shares(table, slots, places, cols, n, examples, chunk, width, rows)
    total = total.reshape(sketch // chunk, chunk // LANES, examples, LANES).transpose(2, 0, 1, 3)
    return total.reshape(examples, sketch) / math.sqrt(sketch)


def solution(mesh):
    placed = (P("grp", None, None), P("grp", None, "feat"), P(), P(), P(), P())
    return jax.shard_map(
        per_device, mesh=mesh, in_specs=placed, out_specs=P("grp", None), check_vma=False
    )
```

```python
import functools
import math

import jax
import jax.numpy as jnp
from jax import lax
from jax.experimental import pallas as pl
from jax.experimental.pallas import tpu as pltpu
from jax.sharding import PartitionSpec as P

BLK = 128
LANES = 128
TILE = 256
CHUNK = 512
F32 = jnp.float32
BF16 = jnp.bfloat16
NT = (((1,), (1,)), ((), ()))
TN = (((0,), (0,)), ((), ()))


def parity(value, bits):
    shift = 1
    while shift < bits:
        shift *= 2
    while shift > 1:
        shift //= 2
        value = value ^ (value >> shift)
    return value & 1


def sign_of(left, right, bits):
    return (1 - 2 * parity(left & right, bits)).astype(F32)


def iota(shape, axis):
    return lax.broadcasted_iota(jnp.int32, shape, axis)


def hits(cols_ref, a, bins, width):
    block = (cols_ref[:, pl.ds(pl.multiple_of(a * TILE, TILE), TILE)] % width) // LANES
    return iota((bins, TILE), 0) == block


def count(cols_ref, rank_ref, start_ref, info_v, bins, width):
    n_rows = cols_ref.shape[1] // TILE
    before = (iota((TILE, 2 * TILE), 0) < iota((TILE, 2 * TILE), 1)).astype(F32).astype(BF16)
    hit = [hits(cols_ref, a, bins, width).astype(F32) for a in range(n_rows)]
    ahead = jnp.dot(
        jnp.concatenate(hit, axis=0).astype(BF16), before, preferred_element_type=F32
    )
    running = jnp.zeros((bins, TILE), F32)
    for a in range(n_rows):
        here = ahead[a * bins : (a + 1) * bins]
        rank = jnp.sum(hit[a] * (here[:, :TILE] + running), axis=0, keepdims=True)
        rank_ref[a : a + 1, :] = rank.astype(jnp.int32)
        running = running + here[:, TILE:]
    need = (running.astype(jnp.int32) + (TILE - 1)) // TILE
    lower = (iota((bins, bins), 1) < iota((bins, bins), 0)).astype(F32).astype(BF16)
    start = jnp.dot(lower, need.astype(F32).astype(BF16), preferred_element_type=F32)
    start_ref[...] = start
    ends = start.astype(jnp.int32) + need
    tile_ids = iota((bins, LANES), 1)
    owner = jnp.sum((ends[:, :LANES] <= tile_ids).astype(jnp.int32), axis=0, keepdims=True)
    owner = jnp.minimum(owner, bins - 1)
    used = ends[bins - 1 :, :LANES]
    info_v[...] = jnp.where(iota((8, LANES), 0) == 0, owner, used)


def place(a, cols_ref, rank_ref, start_ref, tp_ref, lp_ref, bins, width, rows, tiles):
    slots = 2 * tiles
    first = jnp.sum(
        jnp.where(hits(cols_ref, a, bins, width), start_ref[...], 0.0), axis=0, keepdims=True
    )
    rank = rank_ref[pl.ds(a, 1), :]
    lane = rank % TILE
    slot = first.astype(jnp.int32) + rank // TILE + (lane // LANES) * tiles
    lane = lane % LANES
    tp_ref[pl.ds(a, 1), :] = slot
    lp_ref[pl.ds(a, 1), :] = lane
    cols = cols_ref[:, pl.ds(pl.multiple_of(a * TILE, TILE), TILE)]
    row = ((cols // width) % rows).astype(F32)
    col = (cols % LANES).astype(F32)
    here = iota((slots, TILE), 0) == slot
    left = jnp.concatenate([jnp.where(here, row, 0.0), jnp.where(here, col, 0.0)], axis=0)
    right = (iota((LANES, TILE), 0) == lane).astype(F32)
    return lax.dot_general(
        left.astype(BF16), right.astype(BF16), NT, preferred_element_type=F32
    )


def stages(parts, first, last):
    half = first
    while half < last:
        for c in range(len(parts)):
            if not c & half:
                low, high = parts[c], parts[c + half]
                parts[c], parts[c + half] = low + high, low - high
        half *= 2
    return parts


def butterfly(g_ref, t1_ref, work_ref, slot, e, step, steps):
    bins, lanes, rows = g_ref.shape[1:]
    share = lanes // steps
    wide = min(rows, LANES)
    unit = 0
    for j in range(share // 16):
        at = pl.ds(pl.multiple_of(step * share + j * 16, 16), 16)
        for h in range(rows // wide):
            span = slice(h * wide, (h + 1) * wide)
            inner = 8 if bins % 8 == 0 else bins
            for c0 in range(0, bins, inner):
                parts = [g_ref[slot, c0 + c, at, span].astype(F32) for c in range(inner)]
                for c, part in enumerate(stages(parts, 1, inner)):
                    work_ref[unit, c0 + c] = part
            for c0 in range(inner):
                parts = [work_ref[unit, c] for c in range(c0, bins, inner)]
                for c, part in enumerate(stages(parts, 1, len(parts))):
                    t1_ref[c0 + c * inner, e, at, span] = part.astype(BF16)
            unit += 1


def tile_values(t, rc_ref, info_s, t1_ref, so_ref):
    examples, _, rows = t1_ref.shape[1:]
    row = rc_ref[0, pl.ds(t, 1), :]
    col = rc_ref[1, pl.ds(t, 1), :]
    low_ids = iota((16, TILE), 0)
    row_low = sign_of(low_ids, row % 16, 4).astype(BF16)
    high_bits = rows // 16
    row_high = sign_of(iota((max(high_bits, 8), TILE), 0), row // 16, 8).astype(BF16)
    weight = jnp.concatenate([row_low * row_high[h : h + 1] for h in range(high_bits)], axis=0)
    block = t1_ref[info_s[0, t]].reshape(examples * LANES, rows)
    value = jnp.dot(block, weight, preferred_element_type=F32)
    col_low = sign_of(iota((8, TILE), 0), col % 8, 3)
    col_high = sign_of(iota((16, TILE), 0), col // 8, 4)
    for e in range(examples):
        total = jnp.zeros((8, TILE), F32)
        for h in range(16):
            at = e * LANES + h * 8
            total = total + value[at : at + 8] * col_high[h : h + 1]
        so_ref[e, pl.ds(t, 1), :] = jnp.sum(total * col_low, axis=0, keepdims=True)


def entries(a, me, table_ref, tp_ref, lp_ref, cols_ref, n_examples, chunk, width, rows):
    per = chunk // TILE

    def wide(ref):
        return jnp.concatenate([ref[pl.ds(per * a + u, 1), :] for u in range(per)], axis=1)

    pick = (iota((table_ref.shape[1], chunk), 0) == wide(tp_ref)).astype(F32).astype(BF16)
    spread = jnp.dot(table_ref[...], pick, preferred_element_type=F32)
    mine = iota((LANES, chunk), 0) == wide(lp_ref)
    high = cols_ref[:, pl.ds(pl.multiple_of(a * chunk, chunk), chunk)] // (width * rows)
    sign = sign_of(high, me, 16)
    kept = [
        jnp.sum(jnp.where(mine, spread[e * LANES : (e + 1) * LANES], 0.0), axis=0, keepdims=True)
        * sign
        for e in range(n_examples)
    ]
    lines = [
        kept[e][:, q * LANES : (q + 1) * LANES]
        for q in range(chunk // LANES)
        for e in range(n_examples)
    ]
    return jnp.concatenate(lines, axis=0).astype(BF16)


def sketch_kernel(
    tiles, me_ref, x_ref, delta_ref, pattern_ref, rs_ref, cs_ref, cols_ref, table_out, tp_out, lp_out,
    table_ref, tp_ref, lp_ref, dt_ref, cf_ref, g_ref, t1_ref, work_ref, rank_ref, start_ref, pacc_ref, rc_ref, so_ref,
    info_v, info_s, sem, out_sem,
):
    e, nb = pl.program_id(0), pl.program_id(1)
    examples, steps = pl.num_programs(0), pl.num_programs(1)
    bins, lanes, rows = g_ref.shape[1:]
    n_examples = t1_ref.shape[1]
    width = bins * lanes
    tokens, step_cols = x_ref.shape[1:]
    n_steps = width // step_cols
    per = min(rows, BLK)
    bands = rows // per
    step_blocks = step_cols // lanes
    step = e * n_steps + nb
    n_rows = rank_ref.shape[0]
    me = me_ref[0]

    @pl.when(step == 0)
    def _():
        count(cols_ref, rank_ref, start_ref, info_v, bins, width)
        copy = pltpu.make_async_copy(info_v, info_s, sem)
        copy.start()
        pacc_ref[...] = jnp.zeros_like(pacc_ref)
        so_ref[...] = jnp.zeros_like(so_ref)
        for b in range(bands):
            band = pattern_ref[pl.ds(me * rows // BLK + b, 1), :]
            for c in range(bins):
                factor = band[:, c : c + 1] * cs_ref[:, c * lanes : (c + 1) * lanes]
                factor = jnp.broadcast_to(factor.astype(F32) / tokens, (per, lanes))
                cf_ref[c, :, b * per : (b + 1) * per] = factor.T
        copy.wait()

    @pl.when(nb == 0)
    def _():
        span = max(rows, LANES)
        window = rs_ref[:, pl.ds(pl.multiple_of(me * rows // span * span, span), span)]
        own = window[:, :rows]
        for u in range(1, span // rows):
            own = jnp.where(me % (span // rows) == u, window[:, u * rows : (u + 1) * rows], own)
        dt_ref[...] = delta_ref[0] * own.astype(F32).astype(BF16)

    slot = lax.rem(e, 2)
    last = lax.rem(e + n_examples - 1, n_examples)
    butterfly(g_ref, t1_ref, work_ref, 1 - slot, last, nb, n_steps)

    per_step = -(-n_rows // (n_examples * n_steps))
    for u in range(per_step):
        pacc_ref[...] += place(
            step * per_step + u, cols_ref, rank_ref, start_ref, tp_ref, lp_ref, bins, width, rows, tiles
        )

    acc = lax.dot_general(x_ref[0], dt_ref[...], TN, preferred_element_type=F32)
    for c in range(step_blocks):
        block = acc[c * lanes : (c + 1) * lanes] * cf_ref[nb * step_blocks + c]
        g_ref[slot, nb * step_blocks + c] = block.astype(BF16)

    @pl.when(step == examples * steps - 1)
    def _():
        slots_out = pltpu.make_async_copy(tp_ref, tp_out, out_sem.at[0])
        lanes_out = pltpu.make_async_copy(lp_ref, lp_out, out_sem.at[1])
        slots_out.start()
        lanes_out.start()
        for q in range(n_steps):
            butterfly(g_ref, t1_ref, work_ref, slot, e, q, n_steps)
        for v in range(2):
            part = pacc_ref[2 * tiles * v : 2 * tiles * (v + 1)].astype(jnp.int32)
            rc_ref[v] = jnp.concatenate([part[:tiles], part[tiles:]], axis=1)

        def four(s, carry):
            for u in range(4):
                tile_values(s * 4 + u, rc_ref, info_s, t1_ref, so_ref)
            return carry

        lax.fori_loop(0, (info_s[1, 0] + 3) // 4, four, 0)
        for k in range(n_examples):
            one = so_ref[k]
            both = jnp.concatenate([one[:, :LANES], one[:, LANES:]], axis=0)
            table_ref[k * LANES : (k + 1) * LANES] = both.T.astype(BF16)
        table_copy = pltpu.make_async_copy(table_ref, table_out, out_sem.at[2])
        table_copy.start()
        slots_out.wait()
        lanes_out.wait()
        table_copy.wait()


def local_sketch(me, x_acts, delta, pattern, row_signs, col_signs, cols):
    examples, tokens, width = x_acts.shape
    rows = delta.shape[2]
    sketch = cols.shape[1]
    bins = width // LANES
    tiles = sketch // TILE + bins
    step_cols = 1024
    steps = width // step_cols
    n_rows = sketch // TILE
    smem = pl.BlockSpec(memory_space=pltpu.SMEM)
    whole = lambda shape: pl.BlockSpec(shape, lambda e, n: (0,) * len(shape))
    units = LANES // steps // 16 * max(rows // LANES, 1)
    table = (examples * LANES, 2 * tiles)
    places = (n_rows, TILE)
    return pl.pallas_call(
        functools.partial(sketch_kernel, tiles),
        grid=(examples, steps),
        out_shape=[
            jax.ShapeDtypeStruct(table, BF16),
            jax.ShapeDtypeStruct(places, jnp.int32),
            jax.ShapeDtypeStruct(places, jnp.int32),
        ],
        in_specs=[
            smem,
            pl.BlockSpec((1, tokens, step_cols), lambda e, n: (e, 0, n)),
            pl.BlockSpec((1, tokens, rows), lambda e, n: (e, 0, 0)),
            whole(pattern.shape),
            whole(row_signs.shape),
            whole(col_signs.shape),
            whole(cols.shape),
        ],
        out_specs=[pl.BlockSpec(memory_space=pltpu.HBM)] * 3,
        scratch_shapes=[
            pltpu.VMEM(table, BF16),
            pltpu.VMEM(places, jnp.int32),
            pltpu.VMEM(places, jnp.int32),
            pltpu.VMEM((tokens, rows), BF16),
            pltpu.VMEM((bins, LANES, rows), F32),
            pltpu.VMEM((2, bins, LANES, rows), BF16),
            pltpu.VMEM((bins, examples, LANES, rows), BF16),
            pltpu.VMEM((units, bins, 16, min(rows, LANES)), F32),
            pltpu.VMEM(places, jnp.int32),
            pltpu.VMEM((bins, TILE), F32),
            pltpu.VMEM((4 * tiles, LANES), F32),
            pltpu.VMEM((2, tiles, TILE), jnp.int32),
            pltpu.VMEM((examples, tiles, TILE), F32),
            pltpu.VMEM((8, LANES), jnp.int32),
            pltpu.SMEM((8, LANES), jnp.int32),
            pltpu.SemaphoreType.DMA,
            pltpu.SemaphoreType.DMA((3,)),
        ],
        compiler_params=pltpu.CompilerParams(vmem_limit_bytes=60 * 2**20),
        cost_estimate=pl.CostEstimate(
            flops=2 * examples * tokens * width * rows,
            bytes_accessed=2 * examples * tokens * (width + rows),
            transcendentals=0,
        ),
    )(me, x_acts, delta, pattern, row_signs, col_signs, cols)


def sum_kernel(
    n, n_examples, chunk, width, rows, table_ref, tp_ref, lp_ref, cols_ref, out_ref,
    part, recv, send1, recv1, send2, recv2,
):
    me = lax.axis_index("feat")
    chunks = cols_ref.shape[1] // chunk
    pieces = n // chunks
    lines = part.shape[1]
    barrier = pltpu.get_barrier_semaphore()

    def other(o):
        return lax.rem(me + o, n)

    def loop(first, last, step):
        def body(o, carry):
            step(o)
            return carry

        lax.fori_loop(first, last, body, 0)

    def greet(o):
        pl.semaphore_signal(
            barrier, inc=1, device_id={"feat": other(o)}, device_id_type=pl.DeviceIdType.MESH
        )

    def share(src, dst, send_sem, recv_sem, to):
        return pltpu.make_async_remote_copy(
            src_ref=src,
            dst_ref=dst,
            send_sem=send_sem,
            recv_sem=recv_sem,
            device_id={"feat": to},
            device_id_type=pl.DeviceIdType.MESH,
        )

    def chunk_at(o):
        return lax.rem(me // pieces + 1 + o, chunks)

    def compute(o):
        a = chunk_at(o)
        found = entries(
            a, me, table_ref, tp_ref, lp_ref, cols_ref, n_examples, chunk, width, rows
        )
        for p in range(pieces):
            part[a * pieces + p] = found[p * lines : (p + 1) * lines]

    def send(o):
        for p in range(pieces):
            to = chunk_at(o) * pieces + p

            @pl.when(to != me)
            def _():
                share(part.at[to], recv.at[me], send1.at[to], recv1.at[me], to).start()

    def step(o):
        compute(2 * o)
        compute(2 * o + 1)
        send(2 * o)
        send(2 * o + 1)

    loop(1, n, greet)
    compute(0)
    compute(1)
    pl.semaphore_wait(barrier, n - 1)
    send(0)
    send(1)
    loop(1, chunks // 2, step)

    def collect(o, total):
        source = other(n - o)
        share(part.at[source], recv.at[source], send1.at[source], recv1.at[source], source).wait_recv()
        return total + recv[source].astype(F32)

    out_ref[me] = lax.fori_loop(1, n, collect, part[me].astype(F32))

    def spread(o):
        to = other(o)
        share(out_ref.at[me], out_ref.at[me], send2.at[to], recv2.at[me], to).start()

    loop(1, n, spread)

    def finish(o):
        to, source = other(o), other(n - o)
        share(part.at[to], recv.at[me], send1.at[to], recv1.at[me], to).wait_send()
        share(out_ref.at[me], out_ref.at[me], send2.at[to], recv2.at[me], to).wait_send()
        share(out_ref.at[source], out_ref.at[source], send2.at[source], recv2.at[source], source).wait_recv()

    loop(1, n, finish)


def sum_shares(table, slots, places, cols, n, examples, chunk, width, rows):
    vmem = pl.BlockSpec(memory_space=pltpu.VMEM)
    shape = (n, cols.shape[1] // n * examples // LANES, LANES)
    return pl.pallas_call(
        functools.partial(sum_kernel, n, examples, chunk, width, rows),
        out_shape=jax.ShapeDtypeStruct(shape, F32),
        in_specs=[vmem] * 4,
        out_specs=vmem,
        scratch_shapes=[pltpu.VMEM(shape, BF16)] * 2 + [pltpu.SemaphoreType.DMA((n,))] * 4,
        compiler_params=pltpu.CompilerParams(
            collective_id=0, has_side_effects=True, vmem_limit_bytes=32 * 2**20
        ),
    )(table, slots, places, cols)


def per_device(x_acts, delta, pattern, row_signs, col_signs, cols):
    examples, tokens, width = x_acts.shape
    rows = delta.shape[2]
    sketch = cols.shape[0]
    n = lax.axis_size("feat")
    me = lax.axis_index("feat")
    chunk = max(sketch // n, CHUNK)
    cols = cols[None]
    table, slots, places = local_sketch(
        me[None], x_acts, delta, pattern, row_signs[None], col_signs[None], cols
    )
    total = sum_shares(table, slots, places, cols, n, examples, chunk, width, rows)
    total = total.reshape(sketch // chunk, chunk // LANES, examples, LANES).transpose(2, 0, 1, 3)
    return total.reshape(examples, sketch) / math.sqrt(sketch)


def solution(mesh):
    placed = (P("grp", None, None), P("grp", None, "feat"), P(), P(), P(), P())
    return jax.shard_map(
        per_device, mesh=mesh, in_specs=placed, out_specs=P("grp", None), check_vma=False
    )
```

```python
import functools
import math

import jax
import jax.numpy as jnp
from jax import lax
from jax.experimental import pallas as pl
from jax.experimental.pallas import tpu as pltpu
from jax.sharding import PartitionSpec as P

BLK = 128
LANES = 128
TILE = 256
CHUNK = 512
F32 = jnp.float32
BF16 = jnp.bfloat16
NT = (((1,), (1,)), ((), ()))
TN = (((0,), (0,)), ((), ()))


def parity(value, bits):
    shift = 1
    while shift < bits:
        shift *= 2
    while shift > 1:
        shift //= 2
        value = value ^ (value >> shift)
    return value & 1


def sign_of(left, right, bits):
    return (1 - 2 * parity(left & right, bits)).astype(F32)


def iota(shape, axis):
    return lax.broadcasted_iota(jnp.int32, shape, axis)


def hits(cols_ref, a, bins, width):
    block = (cols_ref[:, pl.ds(pl.multiple_of(a * TILE, TILE), TILE)] % width) // LANES
    return iota((bins, TILE), 0) == block


def count(cols_ref, rank_ref, start_ref, info_v, bins, width):
    n_rows = cols_ref.shape[1] // TILE
    before = (iota((TILE, 2 * TILE), 0) < iota((TILE, 2 * TILE), 1)).astype(F32).astype(BF16)
    hit = [hits(cols_ref, a, bins, width).astype(F32) for a in range(n_rows)]
    ahead = jnp.dot(
        jnp.concatenate(hit, axis=0).astype(BF16), before, preferred_element_type=F32
    )
    running = jnp.zeros((bins, TILE), F32)
    for a in range(n_rows):
        here = ahead[a * bins : (a + 1) * bins]
        rank = jnp.sum(hit[a] * (here[:, :TILE] + running), axis=0, keepdims=True)
        rank_ref[a : a + 1, :] = rank.astype(jnp.int32)
        running = running + here[:, TILE:]
    need = (running.astype(jnp.int32) + (TILE - 1)) // TILE
    lower = (iota((bins, bins), 1) < iota((bins, bins), 0)).astype(F32).astype(BF16)
    start = jnp.dot(lower, need.astype(F32).astype(BF16), preferred_element_type=F32)
    start_ref[...] = start
    ends = start.astype(jnp.int32) + need
    tile_ids = iota((bins, LANES), 1)
    owner = jnp.sum((ends[:, :LANES] <= tile_ids).astype(jnp.int32), axis=0, keepdims=True)
    owner = jnp.minimum(owner, bins - 1)
    used = ends[bins - 1 :, :LANES]
    info_v[...] = jnp.where(iota((8, LANES), 0) == 0, owner, used)


def place(a, cols_ref, rank_ref, start_ref, tp_ref, lp_ref, bins, width, rows, tiles):
    slots = 2 * tiles
    first = jnp.sum(
        jnp.where(hits(cols_ref, a, bins, width), start_ref[...], 0.0), axis=0, keepdims=True
    )
    rank = rank_ref[pl.ds(a, 1), :]
    lane = rank % TILE
    slot = first.astype(jnp.int32) + rank // TILE + (lane // LANES) * tiles
    lane = lane % LANES
    tp_ref[pl.ds(a, 1), :] = slot
    lp_ref[pl.ds(a, 1), :] = lane
    cols = cols_ref[:, pl.ds(pl.multiple_of(a * TILE, TILE), TILE)]
    row = ((cols // width) % rows).astype(F32)
    col = (cols % LANES).astype(F32)
    here = iota((slots, TILE), 0) == slot
    left = jnp.concatenate([jnp.where(here, row, 0.0), jnp.where(here, col, 0.0)], axis=0)
    right = (iota((LANES, TILE), 0) == lane).astype(F32)
    return lax.dot_general(
        left.astype(BF16), right.astype(BF16), NT, preferred_element_type=F32
    )


def stages(parts, first, last):
    half = first
    while half < last:
        for c in range(len(parts)):
            if not c & half:
                low, high = parts[c], parts[c + half]
                parts[c], parts[c + half] = low + high, low - high
        half *= 2
    return parts


def butterfly(g_ref, t1_ref, work_ref, slot, e, step, steps):
    bins, lanes, rows = g_ref.shape[1:]
    share = lanes // steps
    wide = min(rows, LANES)
    unit = 0
    for j in range(share // 16):
        at = pl.ds(pl.multiple_of(step * share + j * 16, 16), 16)
        for h in range(rows // wide):
            span = slice(h * wide, (h + 1) * wide)
            inner = 8 if bins % 8 == 0 else bins
            for c0 in range(0, bins, inner):
                parts = [g_ref[slot, c0 + c, at, span].astype(F32) for c in range(inner)]
                for c, part in enumerate(stages(parts, 1, inner)):
                    work_ref[unit, c0 + c] = part
            for c0 in range(inner):
                parts = [work_ref[unit, c] for c in range(c0, bins, inner)]
                for c, part in enumerate(stages(parts, 1, len(parts))):
                    t1_ref[c0 + c * inner, e, at, span] = part.astype(BF16)
            unit += 1


def tile_values(t, rc_ref, info_s, t1_ref, so_ref):
    examples, _, rows = t1_ref.shape[1:]
    row = rc_ref[0, pl.ds(t, 1), :]
    col = rc_ref[1, pl.ds(t, 1), :]
    low_ids = iota((16, TILE), 0)
    row_low = sign_of(low_ids, row % 16, 4).astype(BF16)
    high_bits = rows // 16
    row_high = sign_of(iota((max(high_bits, 8), TILE), 0), row // 16, 8).astype(BF16)
    weight = jnp.concatenate([row_low * row_high[h : h + 1] for h in range(high_bits)], axis=0)
    block = t1_ref[info_s[0, t]].reshape(examples * LANES, rows)
    value = jnp.dot(block, weight, preferred_element_type=F32)
    col_low = sign_of(iota((8, TILE), 0), col % 8, 3)
    col_high = sign_of(iota((16, TILE), 0), col // 8, 4)
    for e in range(examples):
        total = jnp.zeros((8, TILE), F32)
        for h in range(16):
            at = e * LANES + h * 8
            total = total + value[at : at + 8] * col_high[h : h + 1]
        so_ref[e, pl.ds(t, 1), :] = jnp.sum(total * col_low, axis=0, keepdims=True)


def entries(a, me, table_ref, tp_ref, lp_ref, cols_ref, n_examples, chunk, width, rows):
    per = chunk // TILE

    def wide(ref):
        return jnp.concatenate([ref[pl.ds(per * a + u, 1), :] for u in range(per)], axis=1)

    pick = (iota((table_ref.shape[1], chunk), 0) == wide(tp_ref)).astype(F32).astype(BF16)
    spread = jnp.dot(table_ref[...], pick, preferred_element_type=F32)
    mine = iota((LANES, chunk), 0) == wide(lp_ref)
    high = cols_ref[:, pl.ds(pl.multiple_of(a * chunk, chunk), chunk)] // (width * rows)
    sign = sign_of(high, me, 16)
    kept = [
        jnp.sum(jnp.where(mine, spread[e * LANES : (e + 1) * LANES], 0.0), axis=0, keepdims=True)
        * sign
        for e in range(n_examples)
    ]
    lines = [
        kept[e][:, q * LANES : (q + 1) * LANES]
        for q in range(chunk // LANES)
        for e in range(n_examples)
    ]
    return jnp.concatenate(lines, axis=0).astype(BF16)


def sketch_kernel(
    tiles, me_ref, x_ref, delta_ref, pattern_ref, rs_ref, cs_ref, cols_ref, table_out, tp_out, lp_out,
    x_buf, delta_buf, table_ref, tp_ref, lp_ref, dt_ref, cf_ref, g_ref, t1_ref, work_ref, rank_ref,
    start_ref, pacc_ref, rc_ref, so_ref, info_v, info_s, x_sem, delta_sem, info_sem, out_sem,
):
    bins, lanes, rows = g_ref.shape[1:]
    n_examples = t1_ref.shape[1]
    width = bins * lanes
    n_slots, tokens, step_cols = x_buf.shape
    n_steps = width // step_cols
    all_steps = n_examples * n_steps
    per = min(rows, BLK)
    bands = rows // per
    step_blocks = step_cols // lanes
    n_rows = rank_ref.shape[0]
    per_step = -(-n_rows // all_steps)
    me = me_ref[0]

    def fetch(step):
        at = pl.ds(pl.multiple_of(step % n_steps * step_cols, step_cols), step_cols)
        slot = step % n_slots
        return pltpu.make_async_copy(x_ref.at[step // n_steps, :, at], x_buf.at[slot], x_sem.at[slot])

    def fetch_delta(e):
        return pltpu.make_async_copy(delta_ref.at[e], delta_buf.at[e], delta_sem.at[e])

    for step in range(min(n_slots, all_steps)):
        if step % n_steps == 0:
            fetch_delta(step // n_steps).start()
        fetch(step).start()
    for e in range(-(-min(n_slots, all_steps) // n_steps), n_examples):
        fetch_delta(e).start()

    count(cols_ref, rank_ref, start_ref, info_v, bins, width)
    info_copy = pltpu.make_async_copy(info_v, info_s, info_sem)
    info_copy.start()
    pacc_ref[...] = jnp.zeros_like(pacc_ref)
    so_ref[...] = jnp.zeros_like(so_ref)
    for b in range(bands):
        band = pattern_ref[pl.ds(me * rows // BLK + b, 1), :]
        for c in range(bins):
            factor = band[:, c : c + 1] * cs_ref[:, c * lanes : (c + 1) * lanes]
            factor = jnp.broadcast_to(factor.astype(F32) / tokens, (per, lanes))
            cf_ref[c, :, b * per : (b + 1) * per] = factor.T
    span = max(rows, LANES)
    window = rs_ref[:, pl.ds(pl.multiple_of(me * rows // span * span, span), span)]
    own = window[:, :rows]
    for u in range(1, span // rows):
        own = jnp.where(me % (span // rows) == u, window[:, u * rows : (u + 1) * rows], own)
    own = own.astype(F32).astype(BF16)

    def one_step(step, carry):
        e, nb = step // n_steps, step % n_steps
        slot = e % 2

        @pl.when(nb == 0)
        def _():
            fetch_delta(e).wait()
            dt_ref[...] = delta_buf[e] * own

        fetch(step).wait()
        last = (e + n_examples - 1) % n_examples
        butterfly(g_ref, t1_ref, work_ref, 1 - slot, last, nb, n_steps)
        for u in range(per_step):
            pacc_ref[...] += place(
                step * per_step + u, cols_ref, rank_ref, start_ref, tp_ref, lp_ref, bins, width, rows, tiles
            )
        acc = lax.dot_general(x_buf[step % n_slots], dt_ref[...], TN, preferred_element_type=F32)
        for c in range(step_blocks):
            block = acc[c * lanes : (c + 1) * lanes] * cf_ref[nb * step_blocks + c]
            g_ref[slot, nb * step_blocks + c] = block.astype(BF16)

        @pl.when(step + n_slots < all_steps)
        def _():
            fetch(step + n_slots).start()

        return carry

    lax.fori_loop(0, all_steps, one_step, 0)

    slots_out = pltpu.make_async_copy(tp_ref, tp_out, out_sem.at[0])
    lanes_out = pltpu.make_async_copy(lp_ref, lp_out, out_sem.at[1])
    slots_out.start()
    lanes_out.start()
    info_copy.wait()
    for q in range(n_steps):
        butterfly(g_ref, t1_ref, work_ref, (n_examples - 1) % 2, n_examples - 1, q, n_steps)
    for v in range(2):
        part = pacc_ref[2 * tiles * v : 2 * tiles * (v + 1)].astype(jnp.int32)
        rc_ref[v] = jnp.concatenate([part[:tiles], part[tiles:]], axis=1)

    def four(s, carry):
        for u in range(4):
            tile_values(s * 4 + u, rc_ref, info_s, t1_ref, so_ref)
        return carry

    lax.fori_loop(0, (info_s[1, 0] + 3) // 4, four, 0)
    for k in range(n_examples):
        one = so_ref[k]
        both = jnp.concatenate([one[:, :LANES], one[:, LANES:]], axis=0)
        table_ref[k * LANES : (k + 1) * LANES] = both.T.astype(BF16)
    table_copy = pltpu.make_async_copy(table_ref, table_out, out_sem.at[2])
    table_copy.start()
    slots_out.wait()
    lanes_out.wait()
    table_copy.wait()


def local_sketch(me, x_acts, delta, pattern, row_signs, col_signs, cols):
    examples, tokens, width = x_acts.shape
    rows = delta.shape[2]
    sketch = cols.shape[1]
    bins = width // LANES
    tiles = sketch // TILE + bins
    step_cols = 1024
    steps = width // step_cols
    n_rows = sketch // TILE
    smem = pl.BlockSpec(memory_space=pltpu.SMEM)
    hbm = pl.BlockSpec(memory_space=pltpu.HBM)
    vmem = pl.BlockSpec(memory_space=pltpu.VMEM)
    slots = min(8, steps * examples)
    units = LANES // steps // 16 * max(rows // LANES, 1)
    table = (examples * LANES, 2 * tiles)
    places = (n_rows, TILE)
    return pl.pallas_call(
        functools.partial(sketch_kernel, tiles),
        out_shape=[
            jax.ShapeDtypeStruct(table, BF16),
            jax.ShapeDtypeStruct(places, jnp.int32),
            jax.ShapeDtypeStruct(places, jnp.int32),
        ],
        in_specs=[smem, hbm, hbm, vmem, vmem, vmem, vmem],
        out_specs=[hbm] * 3,
        scratch_shapes=[
            pltpu.VMEM((slots, tokens, step_cols), BF16),
            pltpu.VMEM((examples, tokens, rows), BF16),
            pltpu.VMEM(table, BF16),
            pltpu.VMEM(places, jnp.int32),
            pltpu.VMEM(places, jnp.int32),
            pltpu.VMEM((tokens, rows), BF16),
            pltpu.VMEM((bins, LANES, rows), F32),
            pltpu.VMEM((2, bins, LANES, rows), BF16),
            pltpu.VMEM((bins, examples, LANES, rows), BF16),
            pltpu.VMEM((units, bins, 16, min(rows, LANES)), F32),
            pltpu.VMEM(places, jnp.int32),
            pltpu.VMEM((bins, TILE), F32),
            pltpu.VMEM((4 * tiles, LANES), F32),
            pltpu.VMEM((2, tiles, TILE), jnp.int32),
            pltpu.VMEM((examples, tiles, TILE), F32),
            pltpu.VMEM((8, LANES), jnp.int32),
            pltpu.SMEM((8, LANES), jnp.int32),
            pltpu.SemaphoreType.DMA((slots,)),
            pltpu.SemaphoreType.DMA((examples,)),
            pltpu.SemaphoreType.DMA,
            pltpu.SemaphoreType.DMA((3,)),
        ],
        compiler_params=pltpu.CompilerParams(vmem_limit_bytes=60 * 2**20),
        cost_estimate=pl.CostEstimate(
            flops=2 * examples * tokens * width * rows,
            bytes_accessed=2 * examples * tokens * (width + rows),
            transcendentals=0,
        ),
    )(me, x_acts, delta, pattern, row_signs, col_signs, cols)


def sum_kernel(
    n, n_examples, chunk, width, rows, table_in, tp_in, lp_in, cols_ref, out_ref,
    table_ref, tp_ref, lp_ref, part, recv, in_sem, send1, recv1, send2, recv2,
):
    fetches = [
        pltpu.make_async_copy(src, dst, in_sem.at[i])
        for i, (src, dst) in enumerate([(table_in, table_ref), (tp_in, tp_ref), (lp_in, lp_ref)])
    ]
    for fetch in fetches:
        fetch.start()
    me = lax.axis_index("feat")
    chunks = cols_ref.shape[1] // chunk
    pieces = n // chunks
    lines = part.shape[1]
    barrier = pltpu.get_barrier_semaphore()

    def other(o):
        return lax.rem(me + o, n)

    def loop(first, last, step):
        def body(o, carry):
            step(o)
            return carry

        lax.fori_loop(first, last, body, 0)

    def greet(o):
        pl.semaphore_signal(
            barrier, inc=1, device_id={"feat": other(o)}, device_id_type=pl.DeviceIdType.MESH
        )

    def share(src, dst, send_sem, recv_sem, to):
        return pltpu.make_async_remote_copy(
            src_ref=src,
            dst_ref=dst,
            send_sem=send_sem,
            recv_sem=recv_sem,
            device_id={"feat": to},
            device_id_type=pl.DeviceIdType.MESH,
        )

    def chunk_at(o):
        return lax.rem(me // pieces + 1 + o, chunks)

    def compute(o):
        a = chunk_at(o)
        found = entries(
            a, me, table_ref, tp_ref, lp_ref, cols_ref, n_examples, chunk, width, rows
        )
        for p in range(pieces):
            part[a * pieces + p] = found[p * lines : (p + 1) * lines]

    def send(o):
        for p in range(pieces):
            to = chunk_at(o) * pieces + p

            @pl.when(to != me)
            def _():
                share(part.at[to], recv.at[me], send1.at[to], recv1.at[me], to).start()

    def step(o):
        compute(2 * o)
        compute(2 * o + 1)
        send(2 * o)
        send(2 * o + 1)

    loop(1, n, greet)
    for fetch in fetches:
        fetch.wait()
    compute(0)
    compute(1)
    pl.semaphore_wait(barrier, n - 1)
    send(0)
    send(1)
    loop(1, chunks // 2, step)

    def collect(o, total):
        source = other(n - o)
        share(part.at[source], recv.at[source], send1.at[source], recv1.at[source], source).wait_recv()
        return total + recv[source].astype(F32)

    out_ref[me] = lax.fori_loop(1, n, collect, part[me].astype(F32))

    def spread(o):
        to = other(o)
        share(out_ref.at[me], out_ref.at[me], send2.at[to], recv2.at[me], to).start()

    loop(1, n, spread)

    def finish(o):
        to, source = other(o), other(n - o)
        share(part.at[to], recv.at[me], send1.at[to], recv1.at[me], to).wait_send()
        share(out_ref.at[me], out_ref.at[me], send2.at[to], recv2.at[me], to).wait_send()
        share(out_ref.at[source], out_ref.at[source], send2.at[source], recv2.at[source], source).wait_recv()

    loop(1, n, finish)


def sum_shares(table, slots, places, cols, n, examples, chunk, width, rows):
    vmem = pl.BlockSpec(memory_space=pltpu.VMEM)
    shape = (n, cols.shape[1] // n * examples // LANES, LANES)
    return pl.pallas_call(
        functools.partial(sum_kernel, n, examples, chunk, width, rows),
        out_shape=jax.ShapeDtypeStruct(shape, F32),
        in_specs=[pl.BlockSpec(memory_space=pltpu.HBM)] * 3 + [vmem],
        out_specs=vmem,
        scratch_shapes=[
            pltpu.VMEM(table.shape, BF16),
            pltpu.VMEM(slots.shape, jnp.int32),
            pltpu.VMEM(slots.shape, jnp.int32),
            pltpu.VMEM(shape, BF16),
            pltpu.VMEM(shape, BF16),
            pltpu.SemaphoreType.DMA((3,)),
        ]
        + [pltpu.SemaphoreType.DMA((n,))] * 4,
        compiler_params=pltpu.CompilerParams(
            collective_id=0, has_side_effects=True, vmem_limit_bytes=60 * 2**20
        ),
    )(table, slots, places, cols)


def per_device(x_acts, delta, pattern, row_signs, col_signs, cols):
    examples, tokens, width = x_acts.shape
    rows = delta.shape[2]
    sketch = cols.shape[0]
    n = lax.axis_size("feat")
    me = lax.axis_index("feat")
    chunk = max(sketch // n, CHUNK)
    cols = cols[None]
    table, slots, places = local_sketch(
        me[None], x_acts, delta, pattern, row_signs[None], col_signs[None], cols
    )
    total = sum_shares(table, slots, places, cols, n, examples, chunk, width, rows)
    total = total.reshape(sketch // chunk, chunk // LANES, examples, LANES).transpose(2, 0, 1, 3)
    return total.reshape(examples, sketch) / math.sqrt(sketch)


def solution(mesh):
    placed = (P("grp", None, None), P("grp", None, "feat"), P(), P(), P(), P())
    return jax.shard_map(
        per_device, mesh=mesh, in_specs=placed, out_specs=P("grp", None), check_vma=False
    )
```

```python
import functools
import math

import jax
import jax.numpy as jnp
from jax import lax
from jax.experimental import pallas as pl
from jax.experimental.pallas import tpu as pltpu
from jax.sharding import PartitionSpec as P

BLK = 128
LANES = 128
TILE = 256
CHUNK = 512
F32 = jnp.float32
BF16 = jnp.bfloat16
NT = (((1,), (1,)), ((), ()))
TN = (((0,), (0,)), ((), ()))


def parity(value, bits):
    shift = 1
    while shift < bits:
        shift *= 2
    while shift > 1:
        shift //= 2
        value = value ^ (value >> shift)
    return value & 1


def low(value, size):
    return value & (size - 1)


def high(value, size):
    return value >> (size.bit_length() - 1)


def sign_of(left, right, bits):
    return jnp.where(parity(left & right, bits) == 0, 1.0, -1.0)


def iota(shape, axis):
    return lax.broadcasted_iota(jnp.int32, shape, axis)


def hits(cols_ref, a, bins, width):
    cols = cols_ref[:, pl.ds(pl.multiple_of(a * TILE, TILE), TILE)]
    block = high(low(cols, width), LANES)
    return iota((bins, TILE), 0) == block


def count(cols_ref, rank_ref, start_ref, info_v, bins, width):
    n_rows = cols_ref.shape[1] // TILE
    before = (iota((TILE, 2 * TILE), 0) < iota((TILE, 2 * TILE), 1)).astype(F32).astype(BF16)
    hit = [hits(cols_ref, a, bins, width).astype(F32) for a in range(n_rows)]
    ahead = jnp.dot(
        jnp.concatenate(hit, axis=0).astype(BF16), before, preferred_element_type=F32
    )
    running = jnp.zeros((bins, TILE), F32)
    for a in range(n_rows):
        here = ahead[a * bins : (a + 1) * bins]
        rank = jnp.sum(hit[a] * (here[:, :TILE] + running), axis=0, keepdims=True)
        rank_ref[a : a + 1, :] = rank.astype(jnp.int32)
        running = running + here[:, TILE:]
    need = high(running.astype(jnp.int32) + (TILE - 1), TILE)
    lower = (iota((bins, bins), 1) < iota((bins, bins), 0)).astype(F32).astype(BF16)
    start = jnp.dot(lower, need.astype(F32).astype(BF16), preferred_element_type=F32)
    start_ref[...] = start
    ends = start.astype(jnp.int32) + need
    tile_ids = iota((bins, LANES), 1)
    owner = jnp.sum((ends[:, :LANES] <= tile_ids).astype(jnp.int32), axis=0, keepdims=True)
    owner = jnp.minimum(owner, bins - 1)
    used = ends[bins - 1 :, :LANES]
    info_v[...] = jnp.where(iota((8, LANES), 0) == 0, owner, used)


def place(a, cols_ref, rank_ref, start_ref, tp_ref, lp_ref, bins, width, rows, tiles):
    slots = 2 * tiles
    first = jnp.sum(
        jnp.where(hits(cols_ref, a, bins, width), start_ref[...], 0.0), axis=0, keepdims=True
    )
    rank = rank_ref[pl.ds(a, 1), :]
    lane = low(rank, TILE)
    slot = first.astype(jnp.int32) + high(rank, TILE) + high(lane, LANES) * tiles
    lane = low(lane, LANES)
    tp_ref[pl.ds(a, 1), :] = slot
    lp_ref[pl.ds(a, 1), :] = lane
    cols = cols_ref[:, pl.ds(pl.multiple_of(a * TILE, TILE), TILE)]
    row = low(high(cols, width), rows).astype(F32)
    col = low(cols, LANES).astype(F32)
    here = iota((slots, TILE), 0) == slot
    left = jnp.concatenate([jnp.where(here, row, 0.0), jnp.where(here, col, 0.0)], axis=0)
    right = (iota((LANES, TILE), 0) == lane).astype(F32)
    return lax.dot_general(
        left.astype(BF16), right.astype(BF16), NT, preferred_element_type=F32
    )


def stages(parts, first, last):
    half = first
    while half < last:
        for c in range(len(parts)):
            if not c & half:
                low, high = parts[c], parts[c + half]
                parts[c], parts[c + half] = low + high, low - high
        half *= 2
    return parts


def butterfly(g_ref, t1_ref, work_ref, slot, e, step, steps):
    bins, lanes, rows = g_ref.shape[1:]
    share = lanes // steps
    wide = min(rows, LANES)
    unit = 0
    for j in range(share // 16):
        at = pl.ds(pl.multiple_of(step * share + j * 16, 16), 16)
        for h in range(rows // wide):
            span = slice(h * wide, (h + 1) * wide)
            inner = 8 if bins % 8 == 0 else bins
            for c0 in range(0, bins, inner):
                parts = [g_ref[slot, c0 + c, at, span].astype(F32) for c in range(inner)]
                for c, part in enumerate(stages(parts, 1, inner)):
                    work_ref[unit, c0 + c] = part
            for c0 in range(inner):
                parts = [work_ref[unit, c] for c in range(c0, bins, inner)]
                for c, part in enumerate(stages(parts, 1, len(parts))):
                    t1_ref[c0 + c * inner, e, at, span] = part.astype(BF16)
            unit += 1


def tile_values(t, rc_ref, info_s, t1_ref, so_ref):
    examples, _, rows = t1_ref.shape[1:]
    row = rc_ref[0, pl.ds(t, 1), :]
    col = rc_ref[1, pl.ds(t, 1), :]
    low_ids = iota((16, TILE), 0)
    row_low = sign_of(low_ids, low(row, 16), 4).astype(BF16)
    outer = rows // 16
    row_high = sign_of(iota((max(outer, 8), TILE), 0), high(row, 16), outer.bit_length()).astype(BF16)
    weight = jnp.concatenate([row_low * row_high[h : h + 1] for h in range(outer)], axis=0)
    block = t1_ref[info_s[0, t]].reshape(examples * LANES, rows)
    value = jnp.dot(block, weight, preferred_element_type=F32)
    col_low = sign_of(iota((8, TILE), 0), low(col, 8), 3)
    col_high = sign_of(iota((16, TILE), 0), high(col, 8), 4)
    for e in range(examples):
        total = jnp.zeros((8, TILE), F32)
        for h in range(16):
            at = e * LANES + h * 8
            total = total + value[at : at + 8] * col_high[h : h + 1]
        so_ref[e, pl.ds(t, 1), :] = jnp.sum(total * col_low, axis=0, keepdims=True)


def entries(a, me, table_ref, tp_ref, lp_ref, cols_ref, n_examples, chunk, width, rows):
    per = chunk // TILE

    def wide(ref):
        return jnp.concatenate([ref[pl.ds(per * a + u, 1), :] for u in range(per)], axis=1)

    slots = table_ref.shape[1] // 2
    pick = (iota((slots, chunk), 0) == wide(tp_ref)).astype(F32).astype(BF16)
    pick = jnp.concatenate([pick, pick], axis=0)
    spread = jnp.dot(table_ref[...], pick, preferred_element_type=F32)
    mine = iota((LANES, chunk), 0) == wide(lp_ref)
    cols = cols_ref[:, pl.ds(pl.multiple_of(a * chunk, chunk), chunk)]
    sign = sign_of(high(cols, width * rows), me, 16)
    kept = [
        jnp.sum(jnp.where(mine, spread[e * LANES : (e + 1) * LANES], 0.0), axis=0, keepdims=True)
        for e in range(n_examples)
    ]
    kept = jnp.concatenate(kept, axis=0) * sign
    lines = [kept[:, q * LANES : (q + 1) * LANES] for q in range(chunk // LANES)]
    return jnp.concatenate(lines, axis=0)


def sketch_kernel(
    tiles, me_ref, x_ref, delta_ref, pattern_ref, rs_ref, cs_ref, cols_ref, table_out, tp_out, lp_out,
    x_buf, delta_buf, table_ref, tp_ref, lp_ref, dt_ref, cf_ref, g_ref, t1_ref, work_ref, rank_ref,
    start_ref, pacc_ref, rc_ref, so_ref, info_v, info_s, x_sem, delta_sem, info_sem, out_sem,
):
    bins, lanes, rows = g_ref.shape[1:]
    n_examples = t1_ref.shape[1]
    width = bins * lanes
    n_slots, tokens, step_cols = x_buf.shape
    n_steps = width // step_cols
    all_steps = n_examples * n_steps
    per = min(rows, BLK)
    bands = rows // per
    step_blocks = step_cols // lanes
    n_rows = rank_ref.shape[0]
    per_step = -(-n_rows // all_steps)
    me = me_ref[0]

    def fetch(step):
        at = pl.ds(pl.multiple_of(low(step, n_steps) * step_cols, step_cols), step_cols)
        slot = low(step, n_slots)
        return pltpu.make_async_copy(x_ref.at[high(step, n_steps), :, at], x_buf.at[slot], x_sem.at[slot])

    def fetch_delta(e):
        return pltpu.make_async_copy(delta_ref.at[e], delta_buf.at[e], delta_sem.at[e])

    for step in range(min(n_slots, all_steps)):
        if step % n_steps == 0:
            fetch_delta(step // n_steps).start()
        fetch(step).start()
    for e in range(-(-min(n_slots, all_steps) // n_steps), n_examples):
        fetch_delta(e).start()

    count(cols_ref, rank_ref, start_ref, info_v, bins, width)
    info_copy = pltpu.make_async_copy(info_v, info_s, info_sem)
    info_copy.start()
    pacc_ref[...] = jnp.zeros_like(pacc_ref)
    so_ref[...] = jnp.zeros_like(so_ref)
    for b in range(bands):
        band = pattern_ref[pl.ds(high(me * rows, BLK) + b, 1), :]
        for c in range(bins):
            factor = band[:, c : c + 1] * cs_ref[:, c * lanes : (c + 1) * lanes]
            factor = jnp.broadcast_to(factor.astype(F32) / tokens, (per, lanes))
            cf_ref[c, :, b * per : (b + 1) * per] = factor.T
    span = max(rows, LANES)
    window = rs_ref[:, pl.ds(pl.multiple_of(high(me * rows, span) * span, span), span)]
    own = window[:, :rows]
    for u in range(1, span // rows):
        own = jnp.where(low(me, span // rows) == u, window[:, u * rows : (u + 1) * rows], own)
    own = own.astype(F32).astype(BF16)

    def one_step(step, carry):
        e, nb = high(step, n_steps), low(step, n_steps)
        slot = low(e, 2)

        @pl.when(nb == 0)
        def _():
            fetch_delta(e).wait()
            dt_ref[...] = delta_buf[e] * own

        fetch(step).wait()
        last = low(e + n_examples - 1, n_examples)
        butterfly(g_ref, t1_ref, work_ref, 1 - slot, last, nb, n_steps)
        for u in range(per_step):
            pacc_ref[...] += place(
                step * per_step + u, cols_ref, rank_ref, start_ref, tp_ref, lp_ref, bins, width, rows, tiles
            )
        acc = lax.dot_general(x_buf[low(step, n_slots)], dt_ref[...], TN, preferred_element_type=F32)
        for c in range(step_blocks):
            block = acc[c * lanes : (c + 1) * lanes] * cf_ref[nb * step_blocks + c]
            g_ref[slot, nb * step_blocks + c] = block.astype(BF16)

        @pl.when(step + n_slots < all_steps)
        def _():
            fetch(step + n_slots).start()

        return carry

    lax.fori_loop(0, all_steps, one_step, 0)

    slots_out = pltpu.make_async_copy(tp_ref, tp_out, out_sem.at[0])
    lanes_out = pltpu.make_async_copy(lp_ref, lp_out, out_sem.at[1])
    slots_out.start()
    lanes_out.start()
    info_copy.wait()
    for q in range(n_steps):
        butterfly(g_ref, t1_ref, work_ref, (n_examples - 1) % 2, n_examples - 1, q, n_steps)
    for v in range(2):
        part = pacc_ref[2 * tiles * v : 2 * tiles * (v + 1)].astype(jnp.int32)
        rc_ref[v] = jnp.concatenate([part[:tiles], part[tiles:]], axis=1)

    def four(s, carry):
        for u in range(4):
            tile_values(s * 4 + u, rc_ref, info_s, t1_ref, so_ref)
        return carry

    lax.fori_loop(0, high(info_s[1, 0] + 3, 4), four, 0)
    for k in range(n_examples):
        one = so_ref[k]
        both = jnp.concatenate([one[:, :LANES], one[:, LANES:]], axis=0)
        both = both.T
        coarse = both.astype(BF16)
        fine = (both - coarse.astype(F32)).astype(BF16)
        table_ref[k * LANES : (k + 1) * LANES] = jnp.concatenate([coarse, fine], axis=1)
    table_copy = pltpu.make_async_copy(table_ref, table_out, out_sem.at[2])
    table_copy.start()
    slots_out.wait()
    lanes_out.wait()
    table_copy.wait()


def local_sketch(me, x_acts, delta, pattern, row_signs, col_signs, cols):
    examples, tokens, width = x_acts.shape
    rows = delta.shape[2]
    sketch = cols.shape[1]
    bins = width // LANES
    tiles = sketch // TILE + bins
    step_cols = 1024
    steps = width // step_cols
    n_rows = sketch // TILE
    smem = pl.BlockSpec(memory_space=pltpu.SMEM)
    hbm = pl.BlockSpec(memory_space=pltpu.HBM)
    vmem = pl.BlockSpec(memory_space=pltpu.VMEM)
    slots = min(8, steps * examples)
    units = LANES // steps // 16 * max(rows // LANES, 1)
    table = (examples * LANES, 4 * tiles)
    places = (n_rows, TILE)
    return pl.pallas_call(
        functools.partial(sketch_kernel, tiles),
        out_shape=[
            jax.ShapeDtypeStruct(table, BF16),
            jax.ShapeDtypeStruct(places, jnp.int32),
            jax.ShapeDtypeStruct(places, jnp.int32),
        ],
        in_specs=[smem, hbm, hbm, vmem, vmem, vmem, vmem],
        out_specs=[hbm] * 3,
        scratch_shapes=[
            pltpu.VMEM((slots, tokens, step_cols), BF16),
            pltpu.VMEM((examples, tokens, rows), BF16),
            pltpu.VMEM(table, BF16),
            pltpu.VMEM(places, jnp.int32),
            pltpu.VMEM(places, jnp.int32),
            pltpu.VMEM((tokens, rows), BF16),
            pltpu.VMEM((bins, LANES, rows), F32),
            pltpu.VMEM((2, bins, LANES, rows), BF16),
            pltpu.VMEM((bins, examples, LANES, rows), BF16),
            pltpu.VMEM((units, bins, 16, min(rows, LANES)), F32),
            pltpu.VMEM(places, jnp.int32),
            pltpu.VMEM((bins, TILE), F32),
            pltpu.VMEM((4 * tiles, LANES), F32),
            pltpu.VMEM((2, tiles, TILE), jnp.int32),
            pltpu.VMEM((examples, tiles, TILE), F32),
            pltpu.VMEM((8, LANES), jnp.int32),
            pltpu.SMEM((8, LANES), jnp.int32),
            pltpu.SemaphoreType.DMA((slots,)),
            pltpu.SemaphoreType.DMA((examples,)),
            pltpu.SemaphoreType.DMA,
            pltpu.SemaphoreType.DMA((3,)),
        ],
        compiler_params=pltpu.CompilerParams(vmem_limit_bytes=60 * 2**20),
        cost_estimate=pl.CostEstimate(
            flops=2 * examples * tokens * width * rows,
            bytes_accessed=2 * examples * tokens * (width + rows),
            transcendentals=0,
        ),
    )(me, x_acts, delta, pattern, row_signs, col_signs, cols)


def sum_kernel(
    n, n_examples, chunk, width, rows, table_in, tp_in, lp_in, cols_ref, out_ref,
    table_ref, tp_ref, lp_ref, part, recv, in_sem, send1, recv1, send2, recv2,
):
    fetches = [
        pltpu.make_async_copy(src, dst, in_sem.at[i])
        for i, (src, dst) in enumerate([(table_in, table_ref), (tp_in, tp_ref), (lp_in, lp_ref)])
    ]
    for fetch in fetches:
        fetch.start()
    me = lax.axis_index("feat")
    chunks = cols_ref.shape[1] // chunk
    pieces = n // chunks
    lines = part.shape[1]
    barrier = pltpu.get_barrier_semaphore()

    def other(o):
        return lax.rem(me + o, n)

    def loop(first, last, step):
        def body(o, carry):
            step(o)
            return carry

        lax.fori_loop(first, last, body, 0)

    def greet(o):
        pl.semaphore_signal(
            barrier, inc=1, device_id={"feat": other(o)}, device_id_type=pl.DeviceIdType.MESH
        )

    def share(src, dst, send_sem, recv_sem, to):
        return pltpu.make_async_remote_copy(
            src_ref=src,
            dst_ref=dst,
            send_sem=send_sem,
            recv_sem=recv_sem,
            device_id={"feat": to},
            device_id_type=pl.DeviceIdType.MESH,
        )

    def chunk_at(o):
        return lax.rem(me // pieces + 1 + o, chunks)

    def compute(o):
        a = chunk_at(o)
        found = entries(
            a, me, table_ref, tp_ref, lp_ref, cols_ref, n_examples, chunk, width, rows
        )
        for p in range(pieces):
            part[a * pieces + p] = found[p * lines : (p + 1) * lines]

    def send(o):
        for p in range(pieces):
            to = chunk_at(o) * pieces + p

            @pl.when(to != me)
            def _():
                share(part.at[to], recv.at[me], send1.at[to], recv1.at[me], to).start()

    def step(o):
        compute(2 * o)
        compute(2 * o + 1)
        send(2 * o)
        send(2 * o + 1)

    loop(1, n, greet)
    for fetch in fetches:
        fetch.wait()
    compute(0)
    compute(1)
    pl.semaphore_wait(barrier, n - 1)
    send(0)
    send(1)
    loop(1, chunks // 2, step)

    def collect(o, total):
        source = other(n - o)
        share(part.at[source], recv.at[source], send1.at[source], recv1.at[source], source).wait_recv()
        return total + recv[source]

    out_ref[me] = lax.fori_loop(1, n, collect, part[me]).astype(BF16)

    def spread(o):
        to = other(o)
        share(out_ref.at[me], out_ref.at[me], send2.at[to], recv2.at[me], to).start()

    loop(1, n, spread)

    def finish(o):
        to, source = other(o), other(n - o)
        share(part.at[to], recv.at[me], send1.at[to], recv1.at[me], to).wait_send()
        share(out_ref.at[me], out_ref.at[me], send2.at[to], recv2.at[me], to).wait_send()
        share(out_ref.at[source], out_ref.at[source], send2.at[source], recv2.at[source], source).wait_recv()

    loop(1, n, finish)


def sum_shares(table, slots, places, cols, n, examples, chunk, width, rows):
    vmem = pl.BlockSpec(memory_space=pltpu.VMEM)
    shape = (n, cols.shape[1] // n * examples // LANES, LANES)
    return pl.pallas_call(
        functools.partial(sum_kernel, n, examples, chunk, width, rows),
        out_shape=jax.ShapeDtypeStruct(shape, BF16),
        in_specs=[pl.BlockSpec(memory_space=pltpu.HBM)] * 3 + [vmem],
        out_specs=vmem,
        scratch_shapes=[
            pltpu.VMEM(table.shape, BF16),
            pltpu.VMEM(slots.shape, jnp.int32),
            pltpu.VMEM(slots.shape, jnp.int32),
            pltpu.VMEM(shape, F32),
            pltpu.VMEM(shape, F32),
            pltpu.SemaphoreType.DMA((3,)),
        ]
        + [pltpu.SemaphoreType.DMA((n,))] * 4,
        compiler_params=pltpu.CompilerParams(
            collective_id=0, has_side_effects=True, vmem_limit_bytes=32 * 2**20
        ),
    )(table, slots, places, cols)


def per_device(x_acts, delta, pattern, row_signs, col_signs, cols):
    examples, tokens, width = x_acts.shape
    rows = delta.shape[2]
    sketch = cols.shape[0]
    n = lax.axis_size("feat")
    me = lax.axis_index("feat")
    chunk = max(sketch // n, CHUNK)
    cols = cols[None]
    table, slots, places = local_sketch(
        me[None], x_acts, delta, pattern, row_signs[None], col_signs[None], cols
    )
    total = sum_shares(table, slots, places, cols, n, examples, chunk, width, rows)
    total = total.reshape(sketch // chunk, chunk // LANES, examples, LANES).transpose(2, 0, 1, 3)
    return total.reshape(examples, sketch).astype(F32) / math.sqrt(sketch)


def solution(mesh):
    placed = (P("grp", None, None), P("grp", None, "feat"), P(), P(), P(), P())
    return jax.shard_map(
        per_device, mesh=mesh, in_specs=placed, out_specs=P("grp", None), check_vma=False
    )
```

```python
import functools
import math

import jax
import jax.numpy as jnp
from jax import lax
from jax.experimental import pallas as pl
from jax.experimental.pallas import tpu as pltpu
from jax.sharding import PartitionSpec as P

BLK = 128
LANES = 128
TILE = 256
CHUNK = 512
HALVES = 2
F32 = jnp.float32
BF16 = jnp.bfloat16
NT = (((1,), (1,)), ((), ()))
TN = (((0,), (0,)), ((), ()))


def parity(value, bits):
    shift = 1
    while shift < bits:
        shift *= 2
    while shift > 1:
        shift //= 2
        value = value ^ (value >> shift)
    return value & 1


def low(value, size):
    return value & (size - 1)


def high(value, size):
    return value >> (size.bit_length() - 1)


def sign_of(left, right, bits):
    return jnp.where(parity(left & right, bits) == 0, 1.0, -1.0)


def iota(shape, axis):
    return lax.broadcasted_iota(jnp.int32, shape, axis)


def hits(cols_ref, a, bins, width):
    cols = cols_ref[:, pl.ds(pl.multiple_of(a * TILE, TILE), TILE)]
    block = high(low(cols, width), LANES)
    return iota((bins, TILE), 0) == block


def count(cols_ref, rank_ref, start_ref, info_v, bins, width):
    n_rows = cols_ref.shape[1] // TILE
    before = (iota((TILE, 2 * TILE), 0) < iota((TILE, 2 * TILE), 1)).astype(F32).astype(BF16)
    hit = [hits(cols_ref, a, bins, width).astype(F32) for a in range(n_rows)]
    ahead = jnp.dot(
        jnp.concatenate(hit, axis=0).astype(BF16), before, preferred_element_type=F32
    )
    running = jnp.zeros((bins, TILE), F32)
    for a in range(n_rows):
        here = ahead[a * bins : (a + 1) * bins]
        rank = jnp.sum(hit[a] * (here[:, :TILE] + running), axis=0, keepdims=True)
        rank_ref[a : a + 1, :] = rank.astype(jnp.int32)
        running = running + here[:, TILE:]
    need = high(running.astype(jnp.int32) + (TILE - 1), TILE)
    lower = (iota((bins, bins), 1) < iota((bins, bins), 0)).astype(F32).astype(BF16)
    start = jnp.dot(lower, need.astype(F32).astype(BF16), preferred_element_type=F32)
    start_ref[...] = start
    ends = start.astype(jnp.int32) + need
    tile_ids = iota((bins, LANES), 1)
    owner = jnp.sum((ends[:, :LANES] <= tile_ids).astype(jnp.int32), axis=0, keepdims=True)
    owner = jnp.minimum(owner, bins - 1)
    used = ends[bins - 1 :, :LANES]
    info_v[...] = jnp.where(iota((8, LANES), 0) == 0, owner, used)


def place(a, cols_ref, rank_ref, start_ref, tp_ref, lp_ref, bins, width, rows, tiles):
    slots = 2 * tiles
    first = jnp.sum(
        jnp.where(hits(cols_ref, a, bins, width), start_ref[...], 0.0), axis=0, keepdims=True
    )
    rank = rank_ref[pl.ds(a, 1), :]
    lane = low(rank, TILE)
    slot = first.astype(jnp.int32) + high(rank, TILE) + high(lane, LANES) * tiles
    lane = low(lane, LANES)
    tp_ref[pl.ds(a, 1), :] = slot
    lp_ref[pl.ds(a, 1), :] = lane
    cols = cols_ref[:, pl.ds(pl.multiple_of(a * TILE, TILE), TILE)]
    row = low(high(cols, width), rows).astype(F32)
    col = low(cols, LANES).astype(F32)
    here = iota((slots, TILE), 0) == slot
    left = jnp.concatenate([jnp.where(here, row, 0.0), jnp.where(here, col, 0.0)], axis=0)
    right = (iota((LANES, TILE), 0) == lane).astype(F32)
    return lax.dot_general(
        left.astype(BF16), right.astype(BF16), NT, preferred_element_type=F32
    )


def stages(parts, first, last):
    half = first
    while half < last:
        for c in range(len(parts)):
            if not c & half:
                low, high = parts[c], parts[c + half]
                parts[c], parts[c + half] = low + high, low - high
        half *= 2
    return parts


def butterfly(g_ref, t1_ref, work_ref, slot, e, step, steps, unit=0):
    bins, lanes, rows = g_ref.shape[1:]
    share = lanes // steps
    wide = min(rows, LANES)
    for j in range(share // 16):
        at = pl.ds(pl.multiple_of(step * share + j * 16, 16), 16)
        for h in range(rows // wide):
            span = slice(h * wide, (h + 1) * wide)
            inner = 8 if bins % 8 == 0 else bins
            for c0 in range(0, bins, inner):
                parts = [g_ref[slot, c0 + c, at, span].astype(F32) for c in range(inner)]
                for c, part in enumerate(stages(parts, 1, inner)):
                    work_ref[unit, c0 + c] = part
            for c0 in range(inner):
                parts = [work_ref[unit, c] for c in range(c0, bins, inner)]
                for c, part in enumerate(stages(parts, 1, len(parts))):
                    t1_ref[c0 + c * inner, e, at, span] = part.astype(BF16)
            unit += 1


def tile_product(t, rc_ref, info_s, t1_ref):
    examples, _, rows = t1_ref.shape[1:]
    row = rc_ref[0, pl.ds(t, 1), :]
    row_low = sign_of(iota((16, TILE), 0), low(row, 16), 4).astype(BF16)
    outer = rows // 16
    row_high = sign_of(iota((max(outer, 8), TILE), 0), high(row, 16), outer.bit_length()).astype(BF16)
    weight = jnp.concatenate([row_low * row_high[h : h + 1] for h in range(outer)], axis=0)
    block = t1_ref[info_s[0, t]].reshape(examples * LANES, rows)
    return jnp.dot(block, weight, preferred_element_type=F32)


def tile_sums(t, value, rc_ref, so_ref):
    col = rc_ref[1, pl.ds(t, 1), :]
    col_low = sign_of(iota((8, TILE), 0), low(col, 8), 3)
    col_high = sign_of(iota((16, TILE), 0), high(col, 8), 4)
    for e in range(so_ref.shape[0]):
        total = jnp.zeros((8, TILE), F32)
        for h in range(16):
            at = e * LANES + h * 8
            total = total + value[at : at + 8] * col_high[h : h + 1]
        so_ref[e, pl.ds(t, 1), :] = jnp.sum(total * col_low, axis=0, keepdims=True)


def wide_row(ref, a, chunk):
    per = chunk // TILE
    return jnp.concatenate([ref[pl.ds(per * a + u, 1), :] for u in range(per)], axis=1)


def entries(a, table_ref, tp_ref, chunk):
    slots = table_ref.shape[1] // 2
    pick = (iota((slots, chunk), 0) == wide_row(tp_ref, a, chunk)).astype(F32).astype(BF16)
    pick = jnp.concatenate([pick, pick], axis=0)
    return jnp.dot(table_ref[...], pick, preferred_element_type=F32)


def chosen(a, me, spread, lp_ref, cols_ref, n_examples, chunk, width, rows):
    mine = iota((LANES, chunk), 0) == wide_row(lp_ref, a, chunk)
    cols = cols_ref[:, pl.ds(pl.multiple_of(a * chunk, chunk), chunk)]
    sign = sign_of(high(cols, width * rows), me, 16)
    kept = [
        jnp.sum(jnp.where(mine, spread[e * LANES : (e + 1) * LANES], 0.0), axis=0, keepdims=True)
        for e in range(n_examples)
    ]
    kept = jnp.concatenate(kept, axis=0) * sign
    lines = [kept[:, q * LANES : (q + 1) * LANES] for q in range(chunk // LANES)]
    return jnp.concatenate(lines, axis=0)


def sketch_kernel(
    tiles, me_ref, x_ref, delta_ref, pattern_ref, rs_ref, cs_ref, cols_ref, table_out, tp_out, lp_out,
    x_buf, delta_buf, table_ref, tp_ref, lp_ref, dt_ref, cf_ref, g_ref, t1_ref, work_ref, rank_ref,
    start_ref, pacc_ref, rc_ref, so_ref, info_v, info_s, x_sem, delta_sem, info_sem, out_sem,
):
    bins, lanes, rows = g_ref.shape[1:]
    n_examples = t1_ref.shape[1]
    width = bins * lanes
    n_slots, tokens, step_cols = x_buf.shape
    n_steps = width // step_cols
    all_steps = n_examples * n_steps
    per = min(rows, BLK)
    bands = rows // per
    step_blocks = step_cols // lanes
    n_rows = rank_ref.shape[0]
    per_step = -(-n_rows // all_steps)
    me = me_ref[0]

    def fetch(step):
        at = pl.ds(pl.multiple_of(low(step, n_steps) * step_cols, step_cols), step_cols)
        slot = low(step, n_slots)
        return pltpu.make_async_copy(x_ref.at[high(step, n_steps), :, at], x_buf.at[slot], x_sem.at[slot])

    def fetch_delta(e):
        return pltpu.make_async_copy(delta_ref.at[e], delta_buf.at[e], delta_sem.at[e])

    for step in range(min(n_slots, all_steps)):
        if step % n_steps == 0:
            fetch_delta(step // n_steps).start()
        fetch(step).start()
    for e in range(-(-min(n_slots, all_steps) // n_steps), n_examples):
        fetch_delta(e).start()

    count(cols_ref, rank_ref, start_ref, info_v, bins, width)
    info_copy = pltpu.make_async_copy(info_v, info_s, info_sem)
    info_copy.start()
    pacc_ref[...] = jnp.zeros_like(pacc_ref)
    so_ref[...] = jnp.zeros_like(so_ref)
    for b in range(bands):
        band = pattern_ref[pl.ds(high(me * rows, BLK) + b, 1), :]
        for c in range(bins):
            factor = band[:, c : c + 1] * cs_ref[:, c * lanes : (c + 1) * lanes]
            factor = jnp.broadcast_to(factor.astype(F32) / tokens, (per, lanes))
            cf_ref[c, :, b * per : (b + 1) * per] = factor.T
    span = max(rows, LANES)
    window = rs_ref[:, pl.ds(pl.multiple_of(high(me * rows, span) * span, span), span)]
    own = window[:, :rows]
    for u in range(1, span // rows):
        own = jnp.where(low(me, span // rows) == u, window[:, u * rows : (u + 1) * rows], own)
    own = own.astype(F32).astype(BF16)

    def one_step(step, carry):
        e, nb = high(step, n_steps), low(step, n_steps)
        slot = low(e, 2)

        @pl.when(nb == 0)
        def _():
            fetch_delta(e).wait()
            dt_ref[...] = delta_buf[e] * own

        fetch(step).wait()
        last = low(e + n_examples - 1, n_examples)
        x_slot = low(step, n_slots)
        cut = step_cols // HALVES
        for half in range(HALVES):
            acc = lax.dot_general(
                x_buf[x_slot, :, half * cut : (half + 1) * cut], dt_ref[...], TN, preferred_element_type=F32
            )
            butterfly(
                g_ref, t1_ref, work_ref, 1 - slot, last, nb * HALVES + half, n_steps * HALVES,
                half * work_ref.shape[0] // HALVES,
            )
            for u in range(half, per_step, HALVES):
                pacc_ref[...] += place(
                    step * per_step + u, cols_ref, rank_ref, start_ref, tp_ref, lp_ref, bins, width, rows, tiles
                )
            first = nb * step_blocks + half * step_blocks // HALVES
            for c in range(step_blocks // HALVES):
                block = acc[c * lanes : (c + 1) * lanes] * cf_ref[first + c]
                g_ref[slot, first + c] = block.astype(BF16)

        @pl.when(step + n_slots < all_steps)
        def _():
            fetch(step + n_slots).start()

        return carry

    lax.fori_loop(0, all_steps, one_step, 0)

    slots_out = pltpu.make_async_copy(tp_ref, tp_out, out_sem.at[0])
    lanes_out = pltpu.make_async_copy(lp_ref, lp_out, out_sem.at[1])
    slots_out.start()
    lanes_out.start()
    info_copy.wait()
    for q in range(n_steps):
        butterfly(g_ref, t1_ref, work_ref, (n_examples - 1) % 2, n_examples - 1, q, n_steps)
    for v in range(2):
        part = pacc_ref[2 * tiles * v : 2 * tiles * (v + 1)].astype(jnp.int32)
        rc_ref[v] = jnp.concatenate([part[:tiles], part[tiles:]], axis=1)

    def eight(s, carry):
        value = tile_product(s * 8, rc_ref, info_s, t1_ref)
        for u in range(8):
            now = value
            if u < 7:
                value = tile_product(s * 8 + u + 1, rc_ref, info_s, t1_ref)
            tile_sums(s * 8 + u, now, rc_ref, so_ref)
        return carry

    lax.fori_loop(0, high(info_s[1, 0] + 7, 8), eight, 0)
    for k in range(n_examples):
        one = so_ref[k]
        both = jnp.concatenate([one[:, :LANES], one[:, LANES:]], axis=0)
        both = both.T
        coarse = both.astype(BF16)
        fine = (both - coarse.astype(F32)).astype(BF16)
        table_ref[k * LANES : (k + 1) * LANES] = jnp.concatenate([coarse, fine], axis=1)
    table_copy = pltpu.make_async_copy(table_ref, table_out, out_sem.at[2])
    table_copy.start()
    slots_out.wait()
    lanes_out.wait()
    table_copy.wait()


def local_sketch(me, x_acts, delta, pattern, row_signs, col_signs, cols):
    examples, tokens, width = x_acts.shape
    rows = delta.shape[2]
    sketch = cols.shape[1]
    bins = width // LANES
    tiles = sketch // TILE + bins
    step_cols = 1024
    steps = width // step_cols
    n_rows = sketch // TILE
    smem = pl.BlockSpec(memory_space=pltpu.SMEM)
    hbm = pl.BlockSpec(memory_space=pltpu.HBM)
    vmem = pl.BlockSpec(memory_space=pltpu.VMEM)
    slots = min(8, steps * examples)
    units = LANES // steps // 16 * max(rows // LANES, 1)
    table = (examples * LANES, 4 * tiles)
    places = (n_rows, TILE)
    return pl.pallas_call(
        functools.partial(sketch_kernel, tiles),
        out_shape=[
            jax.ShapeDtypeStruct(table, BF16),
            jax.ShapeDtypeStruct(places, jnp.int32),
            jax.ShapeDtypeStruct(places, jnp.int32),
        ],
        in_specs=[smem, hbm, hbm, vmem, vmem, vmem, vmem],
        out_specs=[hbm] * 3,
        scratch_shapes=[
            pltpu.VMEM((slots, tokens, step_cols), BF16),
            pltpu.VMEM((examples, tokens, rows), BF16),
            pltpu.VMEM(table, BF16),
            pltpu.VMEM(places, jnp.int32),
            pltpu.VMEM(places, jnp.int32),
            pltpu.VMEM((tokens, rows), BF16),
            pltpu.VMEM((bins, LANES, rows), F32),
            pltpu.VMEM((2, bins, LANES, rows), BF16),
            pltpu.VMEM((bins, examples, LANES, rows), BF16),
            pltpu.VMEM((units, bins, 16, min(rows, LANES)), F32),
            pltpu.VMEM(places, jnp.int32),
            pltpu.VMEM((bins, TILE), F32),
            pltpu.VMEM((4 * tiles, LANES), F32),
            pltpu.VMEM((2, tiles, TILE), jnp.int32),
            pltpu.VMEM((examples, tiles, TILE), F32),
            pltpu.VMEM((8, LANES), jnp.int32),
            pltpu.SMEM((8, LANES), jnp.int32),
            pltpu.SemaphoreType.DMA((slots,)),
            pltpu.SemaphoreType.DMA((examples,)),
            pltpu.SemaphoreType.DMA,
            pltpu.SemaphoreType.DMA((3,)),
        ],
        compiler_params=pltpu.CompilerParams(vmem_limit_bytes=60 * 2**20),
        cost_estimate=pl.CostEstimate(
            flops=2 * examples * tokens * width * rows,
            bytes_accessed=2 * examples * tokens * (width + rows),
            transcendentals=0,
        ),
    )(me, x_acts, delta, pattern, row_signs, col_signs, cols)


def sum_kernel(
    n, n_examples, chunk, width, rows, table_in, tp_in, lp_in, cols_ref, out_ref,
    table_ref, tp_ref, lp_ref, part, recv, in_sem, send1, recv1, send2, recv2,
):
    fetches = [
        pltpu.make_async_copy(src, dst, in_sem.at[i])
        for i, (src, dst) in enumerate([(table_in, table_ref), (tp_in, tp_ref), (lp_in, lp_ref)])
    ]
    for fetch in fetches:
        fetch.start()
    me = lax.axis_index("feat")
    chunks = cols_ref.shape[1] // chunk
    pieces = n // chunks
    lines = part.shape[1]
    barrier = pltpu.get_barrier_semaphore()

    def other(o):
        return me ^ (n - o)

    def loop(first, last, step):
        def body(o, carry):
            step(o)
            return carry

        lax.fori_loop(first, last, body, 0)

    def greet(o):
        pl.semaphore_signal(
            barrier, inc=1, device_id={"feat": other(o)}, device_id_type=pl.DeviceIdType.MESH
        )

    def share(src, dst, send_sem, recv_sem, to):
        return pltpu.make_async_remote_copy(
            src_ref=src,
            dst_ref=dst,
            send_sem=send_sem,
            recv_sem=recv_sem,
            device_id={"feat": to},
            device_id_type=pl.DeviceIdType.MESH,
        )

    def chunk_at(o):
        return high(me, pieces) ^ (chunks - 1 - o)

    def compute(first):
        spread = [entries(chunk_at(first + u), table_ref, tp_ref, chunk) for u in range(2)]
        for u in range(2):
            a = chunk_at(first + u)
            found = chosen(a, me, spread[u], lp_ref, cols_ref, n_examples, chunk, width, rows)
            for p in range(pieces):
                part[a * pieces + p] = found[p * lines : (p + 1) * lines]

    def send(o):
        for p in range(pieces):
            to = chunk_at(o) * pieces + p

            @pl.when(to != me)
            def _():
                share(part.at[to], recv.at[me], send1.at[to], recv1.at[me], to).start()

    def step(o):
        compute(2 * o)
        send(2 * o)
        send(2 * o + 1)

    loop(1, n, greet)
    for fetch in fetches:
        fetch.wait()
    compute(0)
    pl.semaphore_wait(barrier, n - 1)
    send(0)
    send(1)
    loop(1, chunks // 2, step)

    def collect(o, total):
        source = other(o)
        share(part.at[source], recv.at[source], send1.at[source], recv1.at[source], source).wait_recv()
        return total + recv[source]

    out_ref[me] = lax.fori_loop(1, n, collect, part[me]).astype(BF16)

    def spread(o):
        to = other(o)
        share(out_ref.at[me], out_ref.at[me], send2.at[to], recv2.at[me], to).start()

    loop(1, n, spread)

    def finish(o):
        to, source = other(o), other(o)
        share(part.at[to], recv.at[me], send1.at[to], recv1.at[me], to).wait_send()
        share(out_ref.at[me], out_ref.at[me], send2.at[to], recv2.at[me], to).wait_send()
        share(out_ref.at[source], out_ref.at[source], send2.at[source], recv2.at[source], source).wait_recv()

    loop(1, n, finish)


def sum_shares(table, slots, places, cols, n, examples, chunk, width, rows):
    vmem = pl.BlockSpec(memory_space=pltpu.VMEM)
    shape = (n, cols.shape[1] // n * examples // LANES, LANES)
    return pl.pallas_call(
        functools.partial(sum_kernel, n, examples, chunk, width, rows),
        out_shape=jax.ShapeDtypeStruct(shape, BF16),
        in_specs=[pl.BlockSpec(memory_space=pltpu.HBM)] * 3 + [vmem],
        out_specs=vmem,
        scratch_shapes=[
            pltpu.VMEM(table.shape, BF16),
            pltpu.VMEM(slots.shape, jnp.int32),
            pltpu.VMEM(slots.shape, jnp.int32),
            pltpu.VMEM(shape, F32),
            pltpu.VMEM(shape, F32),
            pltpu.SemaphoreType.DMA((3,)),
        ]
        + [pltpu.SemaphoreType.DMA((n,))] * 4,
        compiler_params=pltpu.CompilerParams(
            collective_id=0, has_side_effects=True, vmem_limit_bytes=60 * 2**20
        ),
    )(table, slots, places, cols)


def per_device(x_acts, delta, pattern, row_signs, col_signs, cols):
    examples, tokens, width = x_acts.shape
    rows = delta.shape[2]
    sketch = cols.shape[0]
    n = lax.axis_size("feat")
    me = lax.axis_index("feat")
    chunk = max(sketch // n, CHUNK)
    cols = cols[None]
    table, slots, places = local_sketch(
        me[None], x_acts, delta, pattern, row_signs[None], col_signs[None], cols
    )
    total = sum_shares(table, slots, places, cols, n, examples, chunk, width, rows)
    total = total.reshape(sketch // chunk, chunk // LANES, examples, LANES).transpose(2, 0, 1, 3)
    return total.reshape(examples, sketch).astype(F32) / math.sqrt(sketch)


def solution(mesh):
    placed = (P("grp", None, None), P("grp", None, "feat"), P(), P(), P(), P())
    return jax.shard_map(
        per_device, mesh=mesh, in_specs=placed, out_specs=P("grp", None), check_vma=False
    )
```

```python
import functools
import math

import jax
import jax.numpy as jnp
from jax import lax
from jax.experimental import pallas as pl
from jax.experimental.pallas import tpu as pltpu
from jax.sharding import PartitionSpec as P

BLK = 128
LANES = 128
TILE = 256
CHUNK = 512
HALVES = 2
F32 = jnp.float32
BF16 = jnp.bfloat16
NT = (((1,), (1,)), ((), ()))


def parity(value, bits):
    shift = 1
    while shift < bits:
        shift *= 2
    while shift > 1:
        shift //= 2
        value = value ^ (value >> shift)
    return value & 1


def low(value, size):
    return value & (size - 1)


def high(value, size):
    return value >> (size.bit_length() - 1)


def sign_of(left, right, bits):
    return jnp.where(parity(left & right, bits) == 0, 1.0, -1.0)


def iota(shape, axis):
    return lax.broadcasted_iota(jnp.int32, shape, axis)


def hits(cols_ref, a, bins, width):
    cols = cols_ref[:, pl.ds(pl.multiple_of(a * TILE, TILE), TILE)]
    block = high(low(cols, width), LANES)
    return iota((bins, TILE), 0) == block


def count(cols_ref, rank_ref, start_ref, info_v, bins, width):
    n_rows = cols_ref.shape[1] // TILE
    before = (iota((TILE, 2 * TILE), 0) < iota((TILE, 2 * TILE), 1)).astype(F32).astype(BF16)
    hit = [hits(cols_ref, a, bins, width).astype(F32) for a in range(n_rows)]
    ahead = jnp.dot(
        jnp.concatenate(hit, axis=0).astype(BF16), before, preferred_element_type=F32
    )
    running = jnp.zeros((bins, TILE), F32)
    for a in range(n_rows):
        here = ahead[a * bins : (a + 1) * bins]
        rank = jnp.sum(hit[a] * (here[:, :TILE] + running), axis=0, keepdims=True)
        rank_ref[a : a + 1, :] = rank.astype(jnp.int32)
        running = running + here[:, TILE:]
    need = high(running.astype(jnp.int32) + (TILE - 1), TILE)
    lower = (iota((bins, bins), 1) < iota((bins, bins), 0)).astype(F32).astype(BF16)
    start = jnp.dot(lower, need.astype(F32).astype(BF16), preferred_element_type=F32)
    start_ref[...] = start
    ends = start.astype(jnp.int32) + need
    tile_ids = iota((bins, LANES), 1)
    owner = jnp.sum((ends[:, :LANES] <= tile_ids).astype(jnp.int32), axis=0, keepdims=True)
    owner = jnp.minimum(owner, bins - 1)
    used = ends[bins - 1 :, :LANES]
    info_v[...] = jnp.where(iota((8, LANES), 0) == 0, owner, used)


def place(a, cols_ref, rank_ref, start_ref, tp_ref, lp_ref, bins, width, rows, tiles):
    slots = 2 * tiles
    first = jnp.sum(
        jnp.where(hits(cols_ref, a, bins, width), start_ref[...], 0.0), axis=0, keepdims=True
    )
    rank = rank_ref[pl.ds(a, 1), :]
    lane = low(rank, TILE)
    slot = first.astype(jnp.int32) + high(rank, TILE) + high(lane, LANES) * tiles
    lane = low(lane, LANES)
    tp_ref[pl.ds(a, 1), :] = slot
    lp_ref[pl.ds(a, 1), :] = lane
    cols = cols_ref[:, pl.ds(pl.multiple_of(a * TILE, TILE), TILE)]
    row = low(high(cols, width), rows).astype(F32)
    col = low(cols, LANES).astype(F32)
    here = iota((slots, TILE), 0) == slot
    left = jnp.concatenate([jnp.where(here, row, 0.0), jnp.where(here, col, 0.0)], axis=0)
    right = (iota((LANES, TILE), 0) == lane).astype(F32)
    return lax.dot_general(
        left.astype(BF16), right.astype(BF16), NT, preferred_element_type=F32
    )


def stages(parts, first, last):
    half = first
    while half < last:
        for c in range(len(parts)):
            if not c & half:
                low, high = parts[c], parts[c + half]
                parts[c], parts[c + half] = low + high, low - high
        half *= 2
    return parts


def butterfly(g_ref, t1_ref, work_ref, slot, e, step, steps, unit=0):
    bins, lanes, rows = g_ref.shape[1:]
    share = lanes // steps
    wide = min(rows, LANES)
    for j in range(share // 16):
        at = pl.ds(pl.multiple_of(step * share + j * 16, 16), 16)
        for h in range(rows // wide):
            span = slice(h * wide, (h + 1) * wide)
            inner = 8 if bins % 8 == 0 else bins
            for c0 in range(0, bins, inner):
                parts = [g_ref[slot, c0 + c, at, span].astype(F32) for c in range(inner)]
                for c, part in enumerate(stages(parts, 1, inner)):
                    work_ref[unit, c0 + c] = part
            for c0 in range(inner):
                parts = [work_ref[unit, c] for c in range(c0, bins, inner)]
                for c, part in enumerate(stages(parts, 1, len(parts))):
                    t1_ref[c0 + c * inner, e, at, span] = part.astype(BF16)
            unit += 1


def tile_product(t, rc_ref, info_s, t1_ref):
    examples, _, rows = t1_ref.shape[1:]
    row = rc_ref[0, pl.ds(t, 1), :]
    row_low = sign_of(iota((16, TILE), 0), low(row, 16), 4).astype(BF16)
    outer = rows // 16
    row_high = sign_of(iota((max(outer, 8), TILE), 0), high(row, 16), outer.bit_length()).astype(BF16)
    weight = jnp.concatenate([row_low * row_high[h : h + 1] for h in range(outer)], axis=0)
    block = t1_ref[info_s[0, t]].reshape(examples * LANES, rows)
    return jnp.dot(block, weight, preferred_element_type=F32)


def tile_sums(t, value, rc_ref, so_ref):
    col = rc_ref[1, pl.ds(t, 1), :]
    col_low = sign_of(iota((8, TILE), 0), low(col, 8), 3)
    col_high = sign_of(iota((16, TILE), 0), high(col, 8), 4)
    for e in range(so_ref.shape[0]):
        total = jnp.zeros((8, TILE), F32)
        for h in range(16):
            at = e * LANES + h * 8
            total = total + value[at : at + 8] * col_high[h : h + 1]
        so_ref[e, pl.ds(t, 1), :] = jnp.sum(total * col_low, axis=0, keepdims=True)


def wide_row(ref, a, chunk):
    per = chunk // TILE
    return jnp.concatenate([ref[pl.ds(per * a + u, 1), :] for u in range(per)], axis=1)


def entries(a, table_ref, tp_ref, chunk):
    slots = table_ref.shape[1] // 2
    pick = (iota((slots, chunk), 0) == wide_row(tp_ref, a, chunk)).astype(F32).astype(BF16)
    pick = jnp.concatenate([pick, pick], axis=0)
    return jnp.dot(table_ref[...], pick, preferred_element_type=F32)


def chosen(a, me, spread, lp_ref, cols_ref, n_examples, chunk, width, rows):
    mine = iota((LANES, chunk), 0) == wide_row(lp_ref, a, chunk)
    cols = cols_ref[:, pl.ds(pl.multiple_of(a * chunk, chunk), chunk)]
    sign = sign_of(high(cols, width * rows), me, 16)
    kept = [
        jnp.sum(jnp.where(mine, spread[e * LANES : (e + 1) * LANES], 0.0), axis=0, keepdims=True)
        for e in range(n_examples)
    ]
    kept = jnp.concatenate(kept, axis=0) * sign
    lines = [kept[:, q * LANES : (q + 1) * LANES] for q in range(chunk // LANES)]
    return jnp.concatenate(lines, axis=0)


def sketch_kernel(
    tiles, me_ref, x_ref, delta_ref, pattern_ref, rs_ref, cs_ref, cols_ref, table_out, tp_out, lp_out,
    x_buf, delta_buf, table_ref, tp_ref, lp_ref, dt_ref, cf_ref, g_ref, t1_ref, work_ref, rank_ref,
    start_ref, pacc_ref, rc_ref, so_ref, info_v, info_s, x_sem, delta_sem, info_sem, out_sem,
):
    bins, lanes, rows = g_ref.shape[1:]
    n_examples = t1_ref.shape[1]
    width = bins * lanes
    n_slots, tokens, step_cols = x_buf.shape
    n_steps = width // step_cols
    all_steps = n_examples * n_steps
    per = min(rows, BLK)
    bands = rows // per
    step_blocks = step_cols // lanes
    n_rows = rank_ref.shape[0]
    per_step = -(-n_rows // all_steps)
    me = me_ref[0]

    def fetch(step):
        at = pl.ds(pl.multiple_of(low(step, n_steps) * step_cols, step_cols), step_cols)
        slot = low(step, n_slots)
        return pltpu.make_async_copy(x_ref.at[high(step, n_steps), :, at], x_buf.at[slot], x_sem.at[slot])

    def fetch_delta(e):
        return pltpu.make_async_copy(delta_ref.at[e], delta_buf.at[e], delta_sem.at[e])

    for step in range(min(n_slots, all_steps)):
        if step % n_steps == 0:
            fetch_delta(step // n_steps).start()
        fetch(step).start()
    for e in range(-(-min(n_slots, all_steps) // n_steps), n_examples):
        fetch_delta(e).start()

    count(cols_ref, rank_ref, start_ref, info_v, bins, width)
    info_copy = pltpu.make_async_copy(info_v, info_s, info_sem)
    info_copy.start()
    pacc_ref[...] = jnp.zeros_like(pacc_ref)
    so_ref[...] = jnp.zeros_like(so_ref)
    for b in range(bands):
        band = pattern_ref[pl.ds(high(me * rows, BLK) + b, 1), :]
        for c in range(bins):
            factor = band[:, c : c + 1] * cs_ref[:, c * lanes : (c + 1) * lanes]
            at = c * lanes % step_cols
            cf_ref[c * lanes // step_cols, b : b + 1, at : at + lanes] = factor.astype(F32) / tokens
    span = max(rows, LANES)
    window = rs_ref[:, pl.ds(pl.multiple_of(high(me * rows, span) * span, span), span)]
    own = window[:, :rows]
    for u in range(1, span // rows):
        own = jnp.where(low(me, span // rows) == u, window[:, u * rows : (u + 1) * rows], own)
    own = own.astype(F32).astype(BF16)

    def one_step(step, carry):
        e, nb = high(step, n_steps), low(step, n_steps)
        slot = low(e, 2)

        @pl.when(nb == 0)
        def _():
            fetch_delta(e).wait()
            dt_ref[...] = (delta_buf[e] * own).T

        fetch(step).wait()
        last = low(e + n_examples - 1, n_examples)
        x_slot = low(step, n_slots)
        cut = step_cols // HALVES
        for half in range(HALVES):
            acc = jnp.dot(
                dt_ref[...], x_buf[x_slot, :, half * cut : (half + 1) * cut], preferred_element_type=F32
            )
            butterfly(
                g_ref, t1_ref, work_ref, 1 - slot, last, nb * HALVES + half, n_steps * HALVES,
                half * work_ref.shape[0] // HALVES,
            )
            for u in range(half, per_step, HALVES):
                pacc_ref[...] += place(
                    step * per_step + u, cols_ref, rank_ref, start_ref, tp_ref, lp_ref, bins, width, rows, tiles
                )
            first = nb * step_blocks + half * step_blocks // HALVES
            factor = cf_ref[nb, :, half * cut : (half + 1) * cut]
            for c in range(step_blocks // HALVES):
                at = slice(c * lanes, (c + 1) * lanes)
                block = [
                    (acc[b * per : (b + 1) * per, at] * factor[b : b + 1, at]).astype(BF16)
                    for b in range(bands)
                ]
                g_ref[slot, first + c] = jnp.concatenate(block, axis=0).T

        @pl.when(step + n_slots < all_steps)
        def _():
            fetch(step + n_slots).start()

        return carry

    lax.fori_loop(0, all_steps, one_step, 0)

    slots_out = pltpu.make_async_copy(tp_ref, tp_out, out_sem.at[0])
    lanes_out = pltpu.make_async_copy(lp_ref, lp_out, out_sem.at[1])
    slots_out.start()
    lanes_out.start()
    info_copy.wait()
    for q in range(n_steps):
        butterfly(g_ref, t1_ref, work_ref, (n_examples - 1) % 2, n_examples - 1, q, n_steps)
    for v in range(2):
        part = pacc_ref[2 * tiles * v : 2 * tiles * (v + 1)].astype(jnp.int32)
        rc_ref[v] = jnp.concatenate([part[:tiles], part[tiles:]], axis=1)

    def eight(s, carry):
        value = tile_product(s * 8, rc_ref, info_s, t1_ref)
        for u in range(8):
            now = value
            if u < 7:
                value = tile_product(s * 8 + u + 1, rc_ref, info_s, t1_ref)
            tile_sums(s * 8 + u, now, rc_ref, so_ref)
        return carry

    lax.fori_loop(0, high(info_s[1, 0] + 7, 8), eight, 0)
    for k in range(n_examples):
        one = so_ref[k]
        both = jnp.concatenate([one[:, :LANES], one[:, LANES:]], axis=0)
        both = both.T
        coarse = both.astype(BF16)
        fine = (both - coarse.astype(F32)).astype(BF16)
        table_ref[k * LANES : (k + 1) * LANES] = jnp.concatenate([coarse, fine], axis=1)
    table_copy = pltpu.make_async_copy(table_ref, table_out, out_sem.at[2])
    table_copy.start()
    slots_out.wait()
    lanes_out.wait()
    table_copy.wait()


def local_sketch(me, x_acts, delta, pattern, row_signs, col_signs, cols):
    examples, tokens, width = x_acts.shape
    rows = delta.shape[2]
    sketch = cols.shape[1]
    bins = width // LANES
    tiles = sketch // TILE + bins
    step_cols = 1024
    steps = width // step_cols
    n_rows = sketch // TILE
    smem = pl.BlockSpec(memory_space=pltpu.SMEM)
    hbm = pl.BlockSpec(memory_space=pltpu.HBM)
    vmem = pl.BlockSpec(memory_space=pltpu.VMEM)
    slots = min(8, steps * examples)
    units = LANES // steps // 16 * max(rows // LANES, 1)
    table = (examples * LANES, 4 * tiles)
    places = (n_rows, TILE)
    return pl.pallas_call(
        functools.partial(sketch_kernel, tiles),
        out_shape=[
            jax.ShapeDtypeStruct(table, BF16),
            jax.ShapeDtypeStruct(places, jnp.int32),
            jax.ShapeDtypeStruct(places, jnp.int32),
        ],
        in_specs=[smem, hbm, hbm, vmem, vmem, vmem, vmem],
        out_specs=[hbm] * 3,
        scratch_shapes=[
            pltpu.VMEM((slots, tokens, step_cols), BF16),
            pltpu.VMEM((examples, tokens, rows), BF16),
            pltpu.VMEM(table, BF16),
            pltpu.VMEM(places, jnp.int32),
            pltpu.VMEM(places, jnp.int32),
            pltpu.VMEM((rows, tokens), BF16),
            pltpu.VMEM((steps, max(rows // BLK, 1), step_cols), F32),
            pltpu.VMEM((2, bins, LANES, rows), BF16),
            pltpu.VMEM((bins, examples, LANES, rows), BF16),
            pltpu.VMEM((units, bins, 16, min(rows, LANES)), F32),
            pltpu.VMEM(places, jnp.int32),
            pltpu.VMEM((bins, TILE), F32),
            pltpu.VMEM((4 * tiles, LANES), F32),
            pltpu.VMEM((2, tiles, TILE), jnp.int32),
            pltpu.VMEM((examples, tiles, TILE), F32),
            pltpu.VMEM((8, LANES), jnp.int32),
            pltpu.SMEM((8, LANES), jnp.int32),
            pltpu.SemaphoreType.DMA((slots,)),
            pltpu.SemaphoreType.DMA((examples,)),
            pltpu.SemaphoreType.DMA,
            pltpu.SemaphoreType.DMA((3,)),
        ],
        compiler_params=pltpu.CompilerParams(vmem_limit_bytes=60 * 2**20),
        cost_estimate=pl.CostEstimate(
            flops=2 * examples * tokens * width * rows,
            bytes_accessed=2 * examples * tokens * (width + rows),
            transcendentals=0,
        ),
    )(me, x_acts, delta, pattern, row_signs, col_signs, cols)


def sum_kernel(
    n, n_examples, chunk, width, rows, table_in, tp_in, lp_in, cols_ref, out_ref,
    table_ref, tp_ref, lp_ref, part, recv, in_sem, send1, recv1, send2, recv2,
):
    fetches = [
        pltpu.make_async_copy(src, dst, in_sem.at[i])
        for i, (src, dst) in enumerate([(table_in, table_ref), (tp_in, tp_ref), (lp_in, lp_ref)])
    ]
    for fetch in fetches:
        fetch.start()
    me = lax.axis_index("feat")
    chunks = cols_ref.shape[1] // chunk
    pieces = n // chunks
    lines = part.shape[1]
    barrier = pltpu.get_barrier_semaphore()

    def other(o):
        return me ^ (n - o)

    def loop(first, last, step):
        def body(o, carry):
            step(o)
            return carry

        lax.fori_loop(first, last, body, 0)

    def greet(o):
        pl.semaphore_signal(
            barrier, inc=1, device_id={"feat": other(o)}, device_id_type=pl.DeviceIdType.MESH
        )

    def share(src, dst, send_sem, recv_sem, to):
        return pltpu.make_async_remote_copy(
            src_ref=src,
            dst_ref=dst,
            send_sem=send_sem,
            recv_sem=recv_sem,
            device_id={"feat": to},
            device_id_type=pl.DeviceIdType.MESH,
        )

    def chunk_at(o):
        return high(me, pieces) ^ (chunks - 1 - o)

    def compute(first):
        spread = [entries(chunk_at(first + u), table_ref, tp_ref, chunk) for u in range(2)]
        for u in range(2):
            a = chunk_at(first + u)
            found = chosen(a, me, spread[u], lp_ref, cols_ref, n_examples, chunk, width, rows)
            for p in range(pieces):
                part[a * pieces + p] = found[p * lines : (p + 1) * lines]

    def send(o):
        for p in range(pieces):
            to = chunk_at(o) * pieces + p

            @pl.when(to != me)
            def _():
                share(part.at[to], recv.at[me], send1.at[to], recv1.at[me], to).start()

    def step(o):
        compute(2 * o)
        send(2 * o)
        send(2 * o + 1)

    loop(1, n, greet)
    for fetch in fetches:
        fetch.wait()
    compute(0)
    pl.semaphore_wait(barrier, n - 1)
    send(0)
    send(1)
    loop(1, chunks // 2, step)

    def collect(o, total):
        source = other(o)
        share(part.at[source], recv.at[source], send1.at[source], recv1.at[source], source).wait_recv()
        return total + recv[source]

    out_ref[me] = lax.fori_loop(1, n, collect, part[me]).astype(BF16)

    def spread(o):
        to = other(o)
        share(out_ref.at[me], out_ref.at[me], send2.at[to], recv2.at[me], to).start()

    loop(1, n, spread)

    def finish(o):
        to, source = other(o), other(o)
        share(part.at[to], recv.at[me], send1.at[to], recv1.at[me], to).wait_send()
        share(out_ref.at[me], out_ref.at[me], send2.at[to], recv2.at[me], to).wait_send()
        share(out_ref.at[source], out_ref.at[source], send2.at[source], recv2.at[source], source).wait_recv()

    loop(1, n, finish)


def sum_shares(table, slots, places, cols, n, examples, chunk, width, rows):
    vmem = pl.BlockSpec(memory_space=pltpu.VMEM)
    shape = (n, cols.shape[1] // n * examples // LANES, LANES)
    return pl.pallas_call(
        functools.partial(sum_kernel, n, examples, chunk, width, rows),
        out_shape=jax.ShapeDtypeStruct(shape, BF16),
        in_specs=[pl.BlockSpec(memory_space=pltpu.HBM)] * 3 + [vmem],
        out_specs=vmem,
        scratch_shapes=[
            pltpu.VMEM(table.shape, BF16),
            pltpu.VMEM(slots.shape, jnp.int32),
            pltpu.VMEM(slots.shape, jnp.int32),
            pltpu.VMEM(shape, F32),
            pltpu.VMEM(shape, F32),
            pltpu.SemaphoreType.DMA((3,)),
        ]
        + [pltpu.SemaphoreType.DMA((n,))] * 4,
        compiler_params=pltpu.CompilerParams(
            collective_id=0, has_side_effects=True, vmem_limit_bytes=60 * 2**20
        ),
    )(table, slots, places, cols)


def per_device(x_acts, delta, pattern, row_signs, col_signs, cols):
    examples, tokens, width = x_acts.shape
    rows = delta.shape[2]
    sketch = cols.shape[0]
    n = lax.axis_size("feat")
    me = lax.axis_index("feat")
    chunk = max(sketch // n, CHUNK)
    cols = cols[None]
    table, slots, places = local_sketch(
        me[None], x_acts, delta, pattern, row_signs[None], col_signs[None], cols
    )
    total = sum_shares(table, slots, places, cols, n, examples, chunk, width, rows)
    total = total.reshape(sketch // chunk, chunk // LANES, examples, LANES).transpose(2, 0, 1, 3)
    return total.reshape(examples, sketch).astype(F32) / math.sqrt(sketch)


def solution(mesh):
    placed = (P("grp", None, None), P("grp", None, "feat"), P(), P(), P(), P())
    return jax.shard_map(
        per_device, mesh=mesh, in_specs=placed, out_specs=P("grp", None), check_vma=False
    )
```
